512 devices in a mesh: grp: 16 (over x, z_hi, core), seq: 32 (over y, z_lo).
Axes of the slice: x: 4, y: 4, z: 16 (z_hi: 2, z_lo: 8; z = z_hi * 8 + z_lo), core: 2. Of those that a mesh axis runs over, the one named last changes fastest.
Arguments:
- x_re: float32 [32, 262144], P(None, ('grp', 'seq')), may hold values from -6 to 6
- x_im: float32 [32, 262144], P(None, ('grp', 'seq')), may hold values from -6 to 6
- gate_in: float32 [32, 262144], P(None, ('grp', 'seq')), may hold values from -6 to 6
- cot_re: float32 [32, 262144], P(None, ('grp', 'seq')), may hold values from -6 to 6
- cot_im: float32 [32, 262144], P(None, ('grp', 'seq')), may hold values from -6 to 6
- filt_re: float32 [32, 512, 512], P('grp', 'seq'), may hold values from -6 to 6
- filt_im: float32 [32, 512, 512], P('grp', 'seq'), may hold values from -6 to 6
Outputs:
- dx_re: float32 [32, 262144], P(None, ('grp', 'seq'))
- dx_im: float32 [32, 262144], P(None, ('grp', 'seq'))
- dgate: float32 [32, 262144], P(None, ('grp', 'seq'))
- dfilt_re: float32 [32, 512, 512], P('grp', 'seq')
- dfilt_im: float32 [32, 512, 512], P('grp', 'seq')
The draws below stay inside these ranges and needn't reach their ends.
All inputs are finite; a program needn't handle non-finite values.
Results may differ from the reference program's by a relative error of at most 0.000098.
Values sent between devices are 32-bit elements; how exact they have to be, the bound alone decides.
A program may use at most 64 MiB of HBM per device.

```python
import jax
import jax.numpy as jnp
from jax import lax

CH = 32
N1 = 512
N2 = 512
SEQ = 262144


def level_of(stream_key, extent, cuts, least, top_value):
    def one(axis_at, parts):
        heights = jax.random.uniform(jax.random.fold_in(jax.random.fold_in(stream_key, 6), axis_at), (parts,), jnp.float32, least / len(cuts), top_value / len(cuts))
        return jnp.repeat(jnp.exp(heights), extent[axis_at] // parts).reshape((-1,) + (1,) * (len(extent) - axis_at - 1))

    level = one(*cuts[0])
    for cut in cuts[1:]:
        level = level * one(*cut)
    return level


def bell_draw(rng, dims, width, most, cuts=(), kind=jnp.bfloat16):
    result = width * jax.random.normal(rng, dims, jnp.float32)
    if cuts:
        result = result * level_of(rng, dims, cuts, -0.22, 0.18)
    return jnp.clip(result, -most, most).astype(kind)


def setup_inputs(seed: int = 0) -> dict:
    seeds = jax.random.split(jax.random.key(seed), 8)
    return {
        "x_re": bell_draw(seeds[0], (CH, SEQ), 1.0, 6.0, ((1, 512),), jnp.float32),
        "x_im": bell_draw(seeds[1], (CH, SEQ), 1.0, 6.0, ((1, 512),), jnp.float32),
        "gate_in": bell_draw(seeds[2], (CH, SEQ), 1.0, 6.0, ((1, 512),), jnp.float32),
        "cot_re": bell_draw(seeds[3], (CH, SEQ), 1.0, 6.0, ((1, 512),), jnp.float32),
        "cot_im": bell_draw(seeds[4], (CH, SEQ), 1.0, 6.0, ((1, 512),), jnp.float32),
        "filt_re": bell_draw(seeds[5], (CH, N1, N2), 1.0, 6.0, ((0, 16), (1, 32)), jnp.float32),
        "filt_im": bell_draw(seeds[6], (CH, N1, N2), 1.0, 6.0, ((0, 16), (1, 32)), jnp.float32),
    }


def reference(x_re, x_im, gate_in, cot_re, cot_im, filt_re, filt_im):
    def one_channel(values):
        real_x, imag_x, gating, real_c, imag_c, resp_re, resp_im = values
        signal = (real_x + 1j * imag_x) * gating
        cotangent = real_c + 1j * imag_c
        response = (resp_re + 1j * resp_im).T.reshape(N1 * N2)
        spec_u = jnp.fft.fft(signal, norm="ortho")
        spec_g = jnp.fft.fft(cotangent, norm="ortho")
        grad_resp = (spec_g * jnp.conj(spec_u)).reshape(N2, N1).T
        grad_sig = jnp.fft.ifft(jnp.conj(response) * spec_g, norm="ortho")
        return (gating * grad_sig.real, gating * grad_sig.imag,
                real_x * grad_sig.real + imag_x * grad_sig.imag,
                grad_resp.real, grad_resp.imag)

    results = lax.map(one_channel, (x_re, x_im, gate_in, cot_re, cot_im, filt_re, filt_im))
    return (results[0], results[1], results[2], results[3], results[4])
```

```python
import functools
import math

import jax
import jax.numpy as jnp
import ml_dtypes
import numpy as np
from jax import lax
from jax.experimental import pallas as pl
from jax.experimental.pallas import tpu as pltpu
from jax.sharding import PartitionSpec as P

N1 = 512
N2 = 512
SEQ = N1 * N2
F32 = jnp.float32
BF16 = jnp.bfloat16
MESH = pl.DeviceIdType.MESH
Z_ORDER = (8, 7, 9, 6, 10, 5, 11, 4, 12, 3, 13, 2, 14, 1, 15)


def split_np(table):
    hi = table.astype(ml_dtypes.bfloat16)
    lo = (table - hi.astype(np.float64)).astype(ml_dtypes.bfloat16)
    return np.stack([hi, lo])


def n_of(p, z):
    return (p // 8) * 128 + (z // 8) * 64 + ((p // 4) % 2) * 32 + (p % 4) * 8 + z % 8


def k1_of(p, r):
    return (p % 4) * 128 + (r // 2) * 16 + (p // 4) * 2 + r % 2


def tables():
    idx = np.arange(512)
    n_rows = n_of(idx // 16, idx % 16)
    k_rows = k1_of(idx // 16, idx % 16)
    k_cols = k1_of((idx % 256) // 8, (idx // 256) * 8 + idx % 8)

    def pair(rows, cols, factor):
        angle = (rows[:, None] * cols[None, :] % 512) * (2.0 * math.pi / 512)
        return np.cos(angle) * factor, np.sin(angle) * factor

    unit = 1.0 / math.sqrt(512.0)

    def by_rows(rows, cols, factor):
        c, s = pair(rows, cols, factor)
        return split_np(np.stack([c.reshape(4, 128, 512), s.reshape(4, 128, 512)], 1).reshape(1024, 512))

    first = by_rows(k_rows, n_rows, 2.0 * unit)
    last = by_rows(n_rows, k_cols, 0.5 * unit)
    c, s = pair(idx, idx, unit)
    mid = split_np(np.stack([c.reshape(512, 4, 128), s.reshape(512, 4, 128)], 2).reshape(512, 1024))
    return first, mid, last


def cross(first, second, bit, size):
    low = jnp.where(bit, pltpu.roll(second, size, 1), first)
    high = jnp.where(bit, second, pltpu.roll(first, 128 - size, 1))
    return low, high


def split(value):
    hi = value.astype(BF16)
    return hi, (value - hi.astype(F32)).astype(BF16)


def dot(a, b):
    return jnp.dot(a, b, preferred_element_type=F32)


def kernel(
    x_re, x_im, gate, cot_re, cot_im, filt_re, filt_im, first_hbm, mid_hbm, last_hbm,
    grad, dfilt,
    vx_re, vx_im, vgate, vcot_re, vcot_im, first, mid, last, tw_cos, tw_sin, bend_cos, bend_sin,
    z_out, z_in, p_in, xx, k_out, k_in, dd, fre, fim, df_out, ee, m_out, m_in, xx2, g_out, g_in, v_out, v_in,
    in_sem, tab_sem, send, recv,
):
    grp = lax.axis_index("grp")
    seq = lax.axis_index("seq")
    x, zh, c = grp // 4, (grp // 2) % 2, grp % 2
    y, zl = seq // 8, seq % 8
    z = zh * 8 + zl
    xc = x * 2 + c
    p = xc * 4 + y
    diag = xc == zl

    def dev(p_to, z_to):
        return ((p_to // 8) * 4 + (z_to // 8) * 2 + (p_to // 4) % 2, (p_to % 4) * 8 + z_to % 8)

    bar = pltpu.get_barrier_semaphore()

    def greet(p_to, z_to):
        pl.semaphore_signal(bar, inc=1, device_id=dev(p_to, z_to), device_id_type=MESH)

    loads = [
        pltpu.make_async_copy(src, dst, in_sem.at[i])
        for i, (src, dst) in enumerate(
            ((x_re, vx_re), (x_im, vx_im), (gate, vgate), (cot_re, vcot_re), (cot_im, vcot_im))
        )
    ]
    for load in loads:
        load.start()
    for off in Z_ORDER:
        greet(p, (z + off) % 16)
    for o in range(8):
        @pl.when(jnp.logical_not(diag & (zl == o)))
        def _():
            greet(zl * 4 + y, zh * 8 + o)
            greet(o * 4 + y, zh * 8 + xc)
    for off in range(31, 0, -1):
        greet(p ^ off, z)
    table_loads = [
        pltpu.make_async_copy(src, dst, tab_sem.at[i])
        for i, (src, dst) in enumerate(((first_hbm, first), (mid_hbm, mid), (last_hbm, last)))
    ]
    for load in table_loads:
        load.start()

    lane = lax.broadcasted_iota(jnp.int32, (32, 128), 1)
    row = lax.broadcasted_iota(jnp.int32, (32, 128), 0)
    bit6 = (lane & 64) != 0
    bit5 = (lane & 32) != 0
    bit4 = (lane & 16) != 0
    odd = (row & 1) != 0

    def pair_swap(v):
        up = pltpu.roll(pltpu.roll(v, 31, 0), 16, 1)
        down = pltpu.roll(pltpu.roll(v, 1, 0), 112, 1)
        return jnp.where(odd == bit4, v, jnp.where(odd, down, up))

    for load in loads:
        load.wait()
    for t in range(4):
        cols = pl.ds(t * 128, 128)
        g = vgate[:, cols]
        a = [vx_re[:, cols] * g, vcot_re[:, cols], vx_im[:, cols] * g, vcot_im[:, cols]]
        b = [None] * 4
        b[0], b[2] = cross(a[0], a[2], bit6, 64)
        b[1], b[3] = cross(a[1], a[3], bit6, 64)
        w = [None] * 4
        w[0], w[1] = cross(b[0], b[1], bit5, 32)
        w[2], w[3] = cross(b[2], b[3], bit5, 32)
        for i in range(4):
            z_out[:, i * 4 + t] = pair_swap(w[i]).reshape(4, 8, 128)

    count = 62 - 2 * diag.astype(jnp.int32)
    pl.semaphore_wait(bar, count)

    def z_rows(z_to):
        return (z_to % 8) // 2, (z_to // 8) * 4 + (z_to % 2) * 2

    for off in Z_ORDER:
        z_to = (z + off) % 16
        tile, sub = z_rows(z_to)
        for w in range(2):
            pltpu.make_async_remote_copy(
                z_out.at[tile, :, sub + w], z_in.at[pl.ds(w * 16, 16), z], send.at[0], recv.at[0],
                device_id=dev(p, z_to), device_id_type=MESH,
            ).start()
    tile, sub = z_rows(z)
    for w in range(2):
        pltpu.make_async_copy(z_out.at[tile, :, sub + w], z_in.at[pl.ds(w * 16, 16), z], recv.at[0]).start()

    for o in range(8):
        for src, dst, got in ((filt_re, fre, 6), (filt_im, fim, 8)):
            there = jnp.logical_not(diag & (zl == o))
            @pl.when(there)
            def _():
                pltpu.make_async_remote_copy(
                    src.at[:, pl.ds(2 * o, 2), :], dst.at[:, pl.ds(2 * zl, 2), :], send.at[6], recv.at[got],
                    device_id=dev(o * 4 + y, zh * 8 + xc), device_id_type=MESH,
                ).start()
            @pl.when(jnp.logical_not(there))
            def _():
                pltpu.make_async_copy(
                    src.at[:, pl.ds(2 * o, 2), :], dst.at[:, pl.ds(2 * zl, 2), :], recv.at[got]
                ).start()

    def angles(k, m):
        return (k * m).astype(F32) * (2.0 * math.pi / SEQ)

    sign = jnp.where(lax.broadcasted_iota(jnp.int32, (128, 128), 1) < 64, 1.0, -1.0).astype(F32)
    m_lane = lax.broadcasted_iota(jnp.int32, (128, 128), 1) % 16 + (
        (p % 4) * 128 + ((p // 4) % 4) * 32 + (p // 16) * 16
    )
    for i in range(4):
        k_row = lax.broadcasted_iota(jnp.int32, (128, 128), 0) + i * 128
        theta = angles(k1_of(k_row // 16, k_row % 16), m_lane)
        tw_cos[pl.ds(i * 128, 128), :] = jnp.cos(theta)
        tw_sin[pl.ds(i * 128, 128), :] = jnp.sin(theta) * sign
        theta = angles(k1_of(p, row % 16), lane + i * 128)
        bend_cos[:, pl.ds(i * 128, 128)] = jnp.cos(theta)
        bend_sin[:, pl.ds(i * 128, 128)] = jnp.sin(theta)

    pltpu.make_async_copy(z_in, z_in, recv.at[0]).wait()

    def plane(src, dst, stage, offs):
        for off in offs:
            pltpu.make_async_remote_copy(
                src.at[p ^ off], dst.at[p], send.at[stage], recv.at[stage],
                device_id=dev(p ^ off, z), device_id_type=MESH,
            ).start()

    def plane_self(src, dst, stage):
        pltpu.make_async_copy(src.at[p], dst.at[p], recv.at[stage]).start()

    plane(z_in, p_in, 1, range(31, 0, -1))
    plane_self(z_in, p_in, 1)
    table_loads[0].wait()
    pltpu.make_async_copy(p_in, p_in, recv.at[1]).wait()

    hi, lo = split(p_in[...].reshape(512, 128))
    xx[:, :128] = hi
    xx[:, 128:] = lo
    for i in range(4):
        chunk = (p // 8) ^ i
        rows = pl.ds(pl.multiple_of(chunk * 256, 256), 256)
        out = dot(first[0, rows, :], xx[...]) + dot(first[1, rows, :], xx[...])
        acc = out[:, :128] + out[:, 128:]
        spec = acc[:128] + sign * pltpu.roll(acc[128:], 64, 1)
        half = pl.ds(pl.multiple_of(chunk * 128, 128), 128)
        turned = spec * tw_cos[half, :] + pltpu.roll(spec, 64, 1) * tw_sin[half, :]
        k_out[pl.ds(chunk * 8, 8)] = turned.reshape(8, 16, 128)
        plane(k_out, k_in, 2, range(i * 8 + (i == 0), i * 8 + 8))
        if i == 0:
            plane_self(k_out, k_in, 2)

    table_loads[1].wait()
    pltpu.make_async_copy(k_in, k_in, recv.at[2]).wait()

    mask6, mask5, mask4 = bit6[:16], bit5[:16], bit4[:16]
    for t in range(4):
        v = {}
        for q in range(8):
            v[q] = k_in[(q & 1) * 16 + (q >> 1) * 4 + t]
        a = {}
        for q in range(4):
            a[q], a[q + 4] = cross(v[q], v[q + 4], mask6, 64)
        b = {}
        for q in (0, 1, 4, 5):
            b[q], b[q + 2] = cross(a[q], a[q + 2], mask5, 32)
        for q in (0, 2, 4, 6):
            d = cross(b[q], b[q + 1], mask4, 16)
            for l in range(2):
                hi, lo = split(d[l])
                dd[pl.ds((q + l) * 16, 16), pl.ds(t * 128, 128)] = hi
                dd[pl.ds(128 + (q + l) * 16, 16), pl.ds(t * 128, 128)] = lo

    pltpu.make_async_copy(fre, fre, recv.at[6]).wait()
    pltpu.make_async_copy(fim, fim, recv.at[8]).wait()
    for i in range(4):
        wide = pl.ds(i * 256, 256)
        cols = pl.ds(i * 128, 128)
        out = dot(dd[...], mid[0, :, wide]) + dot(dd[...], mid[1, :, wide])
        acc = out[:128] + out[128:]
        re = acc[:64, :128] + acc[64:, 128:]
        im = acc[64:, :128] - acc[:64, 128:]
        u_re, g_re, u_im, g_im = re[:32], re[32:], im[:32], im[32:]
        df_out[0, :, :, cols] = (g_re * u_re + g_im * u_im).reshape(2, 16, 128)
        df_out[1, :, :, cols] = (g_im * u_re - g_re * u_im).reshape(2, 16, 128)
        f_re = fre[:, :, cols].reshape(32, 128)
        f_im = fim[:, :, cols].reshape(32, 128)
        hi, lo = split(jnp.concatenate([f_re * g_re + f_im * g_im, f_re * g_im - f_im * g_re], 0))
        ee[:64, cols] = hi
        ee[64:, cols] = lo

    mask5_8, mask4_8 = bit5[:8], bit4[:8]
    for t in range(4):
        wide = pl.ds(t * 256, 256)
        cols = pl.ds(t * 128, 128)
        out = dot(ee[...], mid[0, :, wide]) + dot(ee[...], mid[1, :, wide])
        acc = out[:64] + out[64:]
        re = acc[:32, :128] - acc[32:, 128:]
        im = acc[32:, :128] + acc[:32, 128:]
        b_cos, b_sin = bend_cos[:, cols], bend_sin[:, cols]
        bent = cross(re * b_cos - im * b_sin, im * b_cos + re * b_sin, bit6, 64)
        for w2 in range(2):
            v = bent[w2]
            a = [cross(v[l * 16 : l * 16 + 8], v[l * 16 + 8 : l * 16 + 16], mask5_8, 32) for l in range(2)]
            for w1 in range(2):
                d = cross(a[0][w1], a[1][w1], mask4_8, 16)
                for w0 in range(2):
                    m_out[w0 * 16 + w2 * 8 + w1 * 4 + t] = d[w0]

    plane(m_out, m_in, 3, range(31, 0, -1))
    plane_self(m_out, m_in, 3)

    for o in range(8):
        there = jnp.logical_not(diag & (zl == o))
        @pl.when(there)
        def _():
            pltpu.make_async_remote_copy(
                df_out.at[:, :, pl.ds(2 * o, 2), :], dfilt.at[:, :, pl.ds(2 * xc, 2), :], send.at[7], recv.at[7],
                device_id=dev(zl * 4 + y, zh * 8 + o), device_id_type=MESH,
            ).start()
        @pl.when(jnp.logical_not(there))
        def _():
            pltpu.make_async_copy(
                df_out.at[:, :, pl.ds(2 * o, 2), :], dfilt.at[:, :, pl.ds(2 * xc, 2), :], recv.at[7]
            ).start()

    table_loads[2].wait()
    pltpu.make_async_copy(m_in, m_in, recv.at[3]).wait()

    v = m_in[...].reshape(256, 128)
    wide5 = (lax.broadcasted_iota(jnp.int32, (256, 128), 1) & 32) != 0
    hi, lo = split(jnp.where(wide5, pltpu.roll(v, 32, 1), v))
    xx2[:256, :128] = hi
    xx2[:256, 128:] = lo
    hi, lo = split(jnp.where(wide5, v, pltpu.roll(v, 96, 1)))
    xx2[256:, :128] = hi
    xx2[256:, 128:] = lo
    pick5 = (lax.broadcasted_iota(jnp.int32, (8, 8, 128), 2) & 32) != 0
    for i in range(4):
        chunk = (p // 8) ^ i
        rows = pl.ds(pl.multiple_of(chunk * 256, 256), 256)
        out = dot(last[0, rows, :], xx2[...]) + dot(last[1, rows, :], xx2[...])
        acc = out[:, :128] + out[:, 128:]
        g = (acc[:128] - sign * pltpu.roll(acc[128:], 64, 1)).reshape(8, 2, 8, 128)
        g_out[pl.ds(chunk * 8, 8)] = jnp.where(pick5, g[:, 1], g[:, 0])
        plane(g_out, g_in, 4, range(i * 8 + (i == 0), i * 8 + 8))
        if i == 0:
            plane_self(g_out, g_in, 4)
    pltpu.make_async_copy(g_in, g_in, recv.at[4]).wait()

    for w0 in range(2):
        for w2 in range(2):
            at = w0 * 16 + w2 * 8
            a, b = g_in[pl.ds(at, 4)].reshape(32, 128), g_in[pl.ds(at + 4, 4)].reshape(32, 128)
            low, high = cross(a, b, bit5, 32)
            v_out[0, w0, pl.ds(w2 * 4, 4)] = low.reshape(4, 8, 128)
            v_out[1, w0, pl.ds(w2 * 4, 4)] = high.reshape(4, 8, 128)
    for off in Z_ORDER:
        z_to = (z + off) % 16
        for w in range(2):
            pltpu.make_async_remote_copy(
                v_out.at[z_to // 8, w, :, z_to % 8], v_in.at[tile, :, sub + w], send.at[5], recv.at[5],
                device_id=dev(p, z_to), device_id_type=MESH,
            ).start()
    for w in range(2):
        pltpu.make_async_copy(v_out.at[zh, w, :, zl], v_in.at[tile, :, sub + w], recv.at[5]).start()
    pltpu.make_async_copy(v_in, v_in, recv.at[5]).wait()

    for t in range(4):
        a = [pair_swap(v_in[:, w2 * 4 + t].reshape(32, 128)) for w2 in range(2)]
        re, im = cross(a[0], a[1], bit6, 64)
        grad[0, :, pl.ds(t * 128, 128)] = re
        grad[1, :, pl.ds(t * 128, 128)] = im

    pltpu.make_async_copy(dfilt, dfilt, recv.at[7]).wait()

    def sent(ref, stage):
        pltpu.make_async_copy(ref, ref, send.at[stage]).wait()

    sent(z_in.at[pl.ds(0, 30)], 0)
    sent(p_in.at[pl.ds(0, 31)], 1)
    sent(k_in.at[pl.ds(0, 31)], 2)
    sent(m_in.at[pl.ds(0, 31)], 3)
    sent(g_in.at[pl.ds(0, 31)], 4)
    sent(g_in.at[pl.ds(0, 30)], 5)
    for stage in (6, 7):
        @pl.when(diag)
        def _():
            sent(p_in.at[pl.ds(0, 14)], stage)
        @pl.when(jnp.logical_not(diag))
        def _():
            sent(p_in.at[pl.ds(0, 16)], stage)


def per_device(x_re, x_im, gate_in, cot_re, cot_im, filt_re, filt_im):
    first, mid, last = (jnp.asarray(t) for t in tables())
    vm = pltpu.VMEM
    grad, dfilt = pl.pallas_call(
        kernel,
        out_shape=(
            jax.ShapeDtypeStruct((2, 32, 512), F32),
            jax.ShapeDtypeStruct((2, 2, 16, 512), F32),
        ),
        in_specs=[pl.BlockSpec(memory_space=pl.ANY)] * 10,
        out_specs=[pl.BlockSpec(memory_space=pltpu.VMEM)] * 2,
        scratch_shapes=[
            vm((32, 512), F32), vm((32, 512), F32), vm((32, 512), F32), vm((32, 512), F32), vm((32, 512), F32),
            vm((2, 1024, 512), BF16), vm((2, 512, 1024), BF16), vm((2, 1024, 512), BF16),
            vm((512, 128), F32), vm((512, 128), F32), vm((32, 512), F32), vm((32, 512), F32),
            vm((4, 16, 8, 128), F32), vm((32, 16, 128), F32), vm((32, 16, 128), F32), vm((512, 256), BF16),
            vm((32, 16, 128), F32), vm((32, 16, 128), F32), vm((256, 512), BF16),
            vm((2, 16, 512), F32), vm((2, 16, 512), F32), vm((2, 2, 16, 512), F32), vm((128, 512), BF16),
            vm((32, 8, 128), F32), vm((32, 8, 128), F32), vm((512, 256), BF16),
            vm((32, 8, 128), F32), vm((32, 8, 128), F32), vm((2, 2, 8, 8, 128), F32), vm((4, 8, 8, 128), F32),
            pltpu.SemaphoreType.DMA((5,)), pltpu.SemaphoreType.DMA((3,)),
            pltpu.SemaphoreType.DMA((8,)), pltpu.SemaphoreType.DMA((9,)),
        ],
        name="spectral_backward",
        compiler_params=pltpu.CompilerParams(
            collective_id=0, has_side_effects=True, vmem_limit_bytes=60 * 1024 * 1024
        ),
    )(x_re, x_im, gate_in, cot_re, cot_im, filt_re, filt_im, first, mid, last)
    dx_re = gate_in * grad[0]
    dx_im = gate_in * grad[1]
    dgate = x_re * grad[0] + x_im * grad[1]
    return dx_re, dx_im, dgate, dfilt[0] * 0.25, dfilt[1] * 0.25


def solution(mesh):
    seq_in = P(None, ("grp", "seq"))
    filt = P("grp", "seq", None)
    return jax.shard_map(
        per_device,
        mesh=mesh,
        in_specs=(seq_in,) * 5 + (filt,) * 2,
        out_specs=(seq_in,) * 3 + (filt,) * 2,
        check_vma=False,
    )
```

```python
import functools
import math

import jax
import jax.numpy as jnp
import ml_dtypes
import numpy as np
from jax import lax
from jax.experimental import pallas as pl
from jax.experimental.pallas import tpu as pltpu
from jax.sharding import PartitionSpec as P

N1 = 512
N2 = 512
SEQ = N1 * N2
F32 = jnp.float32
BF16 = jnp.bfloat16
MESH = pl.DeviceIdType.MESH
Z_ORDER = (8, 7, 9, 6, 10, 5, 11, 4, 12, 3, 13, 2, 14, 1, 15)


def split_np(table):
    hi = table.astype(ml_dtypes.bfloat16)
    lo = (table - hi.astype(np.float64)).astype(ml_dtypes.bfloat16)
    return np.stack([hi, lo])


def n_of(p, z):
    return (p // 8) * 128 + (z // 8) * 64 + ((p // 4) % 2) * 32 + (p % 4) * 8 + z % 8


def k1_of(p, r):
    return (p % 4) * 128 + (r // 2) * 16 + (p // 4) * 2 + r % 2


def tables():
    idx = np.arange(512)
    n_rows = n_of(idx // 16, idx % 16)
    k_rows = k1_of(idx // 16, idx % 16)
    k_cols = k1_of((idx % 256) // 8, (idx // 256) * 8 + idx % 8)

    def pair(rows, cols, factor):
        angle = (rows[:, None] * cols[None, :] % 512) * (2.0 * math.pi / 512)
        return np.cos(angle) * factor, np.sin(angle) * factor

    unit = 1.0 / math.sqrt(512.0)

    def by_rows(rows, cols, factor):
        c, s = pair(rows, cols, factor)
        return split_np(np.stack([c.reshape(4, 128, 512), s.reshape(4, 128, 512)], 1).reshape(1024, 512))

    first = by_rows(k_rows, n_rows, 2.0 * unit)
    last = by_rows(n_rows, k_cols, 0.5 * unit)
    c, s = pair(idx, idx, unit)
    mid = split_np(np.stack([c.reshape(512, 4, 128), s.reshape(512, 4, 128)], 2).reshape(512, 1024))
    return first, mid, last


def cross(first, second, bit, size):
    low = jnp.where(bit, pltpu.roll(second, size, 1), first)
    high = jnp.where(bit, second, pltpu.roll(first, 128 - size, 1))
    return low, high


def split(value):
    hi = value.astype(BF16)
    return hi, (value - hi.astype(F32)).astype(BF16)


def dot(a, b):
    return jnp.dot(a, b, preferred_element_type=F32)


def kernel(
    x_re, x_im, gate, cot_re, cot_im, filt_re, filt_im, first_hbm, mid_hbm, last_hbm,
    outs,
    vx_re, vx_im, vgate, vcot_re, vcot_im, first, mid, last, tw_cos, tw_sin, bend_cos, bend_sin,
    z_out, z_in, p_in, xx, k_out, k_in, dd, f_mid, f_in, df_out, df_mid, ee, m_out, m_in, xx2, g_out, g_in, v_out, v_in, dfilt,
    in_sem, tab_sem, send, recv,
):
    grp = lax.axis_index("grp")
    seq = lax.axis_index("seq")
    x, zh, c = grp // 4, (grp // 2) % 2, grp % 2
    y, zl = seq // 8, seq % 8
    z = zh * 8 + zl
    xc = x * 2 + c
    p = xc * 4 + y

    def dev(p_to, z_to):
        return ((p_to // 8) * 4 + (z_to // 8) * 2 + (p_to // 4) % 2, (p_to % 4) * 8 + z_to % 8)

    bar = pltpu.get_barrier_semaphore()

    def greet(p_to, z_to):
        pl.semaphore_signal(bar, inc=1, device_id=dev(p_to, z_to), device_id_type=MESH)

    loads = [
        pltpu.make_async_copy(src, dst, in_sem.at[i])
        for i, (src, dst) in enumerate(
            ((x_re, vx_re), (x_im, vx_im), (gate, vgate), (cot_re, vcot_re), (cot_im, vcot_im))
        )
    ]
    for load in loads:
        load.start()
    for off in Z_ORDER:
        greet(p, (z + off) % 16)
    for off in range(31, 0, -1):
        greet(p ^ off, z)
    table_loads = [
        pltpu.make_async_copy(src, dst, tab_sem.at[i])
        for i, (src, dst) in enumerate(((first_hbm, first), (mid_hbm, mid), (last_hbm, last)))
    ]
    for load in table_loads:
        load.start()

    lane = lax.broadcasted_iota(jnp.int32, (32, 128), 1)
    row = lax.broadcasted_iota(jnp.int32, (32, 128), 0)
    bit6 = (lane & 64) != 0
    bit5 = (lane & 32) != 0
    bit4 = (lane & 16) != 0
    odd = (row & 1) != 0

    def pair_swap(v):
        up = pltpu.roll(pltpu.roll(v, 31, 0), 16, 1)
        down = pltpu.roll(pltpu.roll(v, 1, 0), 112, 1)
        return jnp.where(odd == bit4, v, jnp.where(odd, down, up))

    for load in loads:
        load.wait()
    for t in range(4):
        cols = pl.ds(t * 128, 128)
        g = vgate[:, cols]
        a = [vx_re[:, cols] * g, vcot_re[:, cols], vx_im[:, cols] * g, vcot_im[:, cols]]
        b = [None] * 4
        b[0], b[2] = cross(a[0], a[2], bit6, 64)
        b[1], b[3] = cross(a[1], a[3], bit6, 64)
        w = [None] * 4
        w[0], w[1] = cross(b[0], b[1], bit5, 32)
        w[2], w[3] = cross(b[2], b[3], bit5, 32)
        for i in range(4):
            z_out[:, i * 4 + t] = pair_swap(w[i]).reshape(4, 8, 128)

    pl.semaphore_wait(bar, 46)

    def z_rows(z_to):
        return (z_to % 8) // 2, (z_to // 8) * 4 + (z_to % 2) * 2

    for off in Z_ORDER:
        z_to = (z + off) % 16
        tile, sub = z_rows(z_to)
        for w in range(2):
            pltpu.make_async_remote_copy(
                z_out.at[tile, :, sub + w], z_in.at[pl.ds(w * 16, 16), z], send.at[0], recv.at[0],
                device_id=dev(p, z_to), device_id_type=MESH,
            ).start()
    tile, sub = z_rows(z)
    for w in range(2):
        pltpu.make_async_copy(z_out.at[tile, :, sub + w], z_in.at[pl.ds(w * 16, 16), z], recv.at[0]).start()

    def spread_plane(pairs, stage):
        for off in (7, 5, 3, 6, 4, 2, 1):
            for src, dst in pairs:
                pltpu.make_async_remote_copy(
                    src.at[..., pl.ds(2 * (xc ^ off), 2), :], dst.at[..., pl.ds(2 * xc, 2), :],
                    send.at[stage], recv.at[stage], device_id=dev(p ^ (off * 4), z), device_id_type=MESH,
                ).start()
        for src, dst in pairs:
            pltpu.make_async_copy(
                src.at[..., pl.ds(2 * xc, 2), :], dst.at[..., pl.ds(2 * xc, 2), :], recv.at[stage]
            ).start()

    def spread_line(src, dst, stage):
        for off in range(7, 0, -1):
            pltpu.make_async_remote_copy(
                src.at[..., pl.ds(2 * (zl ^ off), 2), :], dst.at[..., pl.ds(2 * zl, 2), :],
                send.at[stage], recv.at[stage], device_id=dev(p, z ^ off), device_id_type=MESH,
            ).start()
        pltpu.make_async_copy(
            src.at[..., pl.ds(2 * zl, 2), :], dst.at[..., pl.ds(2 * zl, 2), :], recv.at[stage]
        ).start()

    spread_plane(((filt_re, f_mid.at[0]), (filt_im, f_mid.at[1])), 6)

    def angles(k, m):
        return (k * m).astype(F32) * (2.0 * math.pi / SEQ)

    sign = jnp.where(lax.broadcasted_iota(jnp.int32, (128, 128), 1) < 64, 1.0, -1.0).astype(F32)
    m_lane = lax.broadcasted_iota(jnp.int32, (128, 128), 1) % 16 + (
        (p % 4) * 128 + ((p // 4) % 4) * 32 + (p // 16) * 16
    )
    for i in range(4):
        k_row = lax.broadcasted_iota(jnp.int32, (128, 128), 0) + i * 128
        theta = angles(k1_of(k_row // 16, k_row % 16), m_lane)
        tw_cos[pl.ds(i * 128, 128), :] = jnp.cos(theta)
        tw_sin[pl.ds(i * 128, 128), :] = jnp.sin(theta) * sign
        theta = angles(k1_of(p, row % 16), lane + i * 128)
        bend_cos[:, pl.ds(i * 128, 128)] = jnp.cos(theta)
        bend_sin[:, pl.ds(i * 128, 128)] = jnp.sin(theta)

    pltpu.make_async_copy(z_in, z_in, recv.at[0]).wait()

    def plane(src, dst, stage, offs):
        for off in offs:
            pltpu.make_async_remote_copy(
                src.at[p ^ off], dst.at[p], send.at[stage], recv.at[stage],
                device_id=dev(p ^ off, z), device_id_type=MESH,
            ).start()

    def plane_self(src, dst, stage):
        pltpu.make_async_copy(src.at[p], dst.at[p], recv.at[stage]).start()

    plane(z_in, p_in, 1, range(31, 0, -1))
    plane_self(z_in, p_in, 1)
    pltpu.make_async_copy(f_mid, f_mid, recv.at[6]).wait()
    spread_line(f_mid, f_in, 7)
    table_loads[0].wait()
    pltpu.make_async_copy(p_in, p_in, recv.at[1]).wait()

    hi, lo = split(p_in[...].reshape(512, 128))
    xx[:, :128] = hi
    xx[:, 128:] = lo
    for i in range(4):
        chunk = (p // 8) ^ i
        rows = pl.ds(pl.multiple_of(chunk * 256, 256), 256)
        out = dot(first[0, rows, :], xx[...]) + dot(first[1, rows, :], xx[...])
        acc = out[:, :128] + out[:, 128:]
        spec = acc[:128] + sign * pltpu.roll(acc[128:], 64, 1)
        half = pl.ds(pl.multiple_of(chunk * 128, 128), 128)
        turned = spec * tw_cos[half, :] + pltpu.roll(spec, 64, 1) * tw_sin[half, :]
        k_out[pl.ds(chunk * 8, 8)] = turned.reshape(8, 16, 128)
        plane(k_out, k_in, 2, range(i * 8 + (i == 0), i * 8 + 8))
        if i == 0:
            plane_self(k_out, k_in, 2)

    table_loads[1].wait()
    pltpu.make_async_copy(k_in, k_in, recv.at[2]).wait()

    mask6, mask5, mask4 = bit6[:16], bit5[:16], bit4[:16]
    for t in range(4):
        v = {}
        for q in range(8):
            v[q] = k_in[(q & 1) * 16 + (q >> 1) * 4 + t]
        a = {}
        for q in range(4):
            a[q], a[q + 4] = cross(v[q], v[q + 4], mask6, 64)
        b = {}
        for q in (0, 1, 4, 5):
            b[q], b[q + 2] = cross(a[q], a[q + 2], mask5, 32)
        for q in (0, 2, 4, 6):
            d = cross(b[q], b[q + 1], mask4, 16)
            for l in range(2):
                hi, lo = split(d[l])
                dd[pl.ds((q + l) * 16, 16), pl.ds(t * 128, 128)] = hi
                dd[pl.ds(128 + (q + l) * 16, 16), pl.ds(t * 128, 128)] = lo

    pltpu.make_async_copy(f_in, f_in, recv.at[7]).wait()
    for i in range(4):
        wide = pl.ds(i * 256, 256)
        cols = pl.ds(i * 128, 128)
        out = dot(dd[...], mid[0, :, wide]) + dot(dd[...], mid[1, :, wide])
        acc = out[:128] + out[128:]
        re = acc[:64, :128] + acc[64:, 128:]
        im = acc[64:, :128] - acc[:64, 128:]
        u_re, g_re, u_im, g_im = re[:32], re[32:], im[:32], im[32:]
        df_out[0, :, :, cols] = (g_re * u_re + g_im * u_im).reshape(2, 16, 128)
        df_out[1, :, :, cols] = (g_im * u_re - g_re * u_im).reshape(2, 16, 128)
        f_re = f_in[0, :, :, cols].reshape(32, 128)
        f_im = f_in[1, :, :, cols].reshape(32, 128)
        hi, lo = split(jnp.concatenate([f_re * g_re + f_im * g_im, f_re * g_im - f_im * g_re], 0))
        ee[:64, cols] = hi
        ee[64:, cols] = lo
    spread_line(df_out, df_mid, 8)

    mask5_8, mask4_8 = bit5[:8], bit4[:8]
    for t in range(4):
        wide = pl.ds(t * 256, 256)
        cols = pl.ds(t * 128, 128)
        out = dot(ee[...], mid[0, :, wide]) + dot(ee[...], mid[1, :, wide])
        acc = out[:64] + out[64:]
        re = acc[:32, :128] - acc[32:, 128:]
        im = acc[32:, :128] + acc[:32, 128:]
        b_cos, b_sin = bend_cos[:, cols], bend_sin[:, cols]
        bent = cross(re * b_cos - im * b_sin, im * b_cos + re * b_sin, bit6, 64)
        for w2 in range(2):
            v = bent[w2]
            a = [cross(v[l * 16 : l * 16 + 8], v[l * 16 + 8 : l * 16 + 16], mask5_8, 32) for l in range(2)]
            for w1 in range(2):
                d = cross(a[0][w1], a[1][w1], mask4_8, 16)
                for w0 in range(2):
                    m_out[w0 * 16 + w2 * 8 + w1 * 4 + t] = d[w0]

    plane(m_out, m_in, 3, range(31, 0, -1))
    plane_self(m_out, m_in, 3)

    table_loads[2].wait()
    pltpu.make_async_copy(m_in, m_in, recv.at[3]).wait()

    v = m_in[...].reshape(256, 128)
    wide5 = (lax.broadcasted_iota(jnp.int32, (256, 128), 1) & 32) != 0
    hi, lo = split(jnp.where(wide5, pltpu.roll(v, 32, 1), v))
    xx2[:256, :128] = hi
    xx2[:256, 128:] = lo
    hi, lo = split(jnp.where(wide5, v, pltpu.roll(v, 96, 1)))
    xx2[256:, :128] = hi
    xx2[256:, 128:] = lo
    pick5 = (lax.broadcasted_iota(jnp.int32, (8, 8, 128), 2) & 32) != 0
    for i in range(4):
        chunk = (p // 8) ^ i
        rows = pl.ds(pl.multiple_of(chunk * 256, 256), 256)
        out = dot(last[0, rows, :], xx2[...]) + dot(last[1, rows, :], xx2[...])
        acc = out[:, :128] + out[:, 128:]
        g = (acc[:128] - sign * pltpu.roll(acc[128:], 64, 1)).reshape(8, 2, 8, 128)
        g_out[pl.ds(chunk * 8, 8)] = jnp.where(pick5, g[:, 1], g[:, 0])
        plane(g_out, g_in, 4, range(i * 8 + (i == 0), i * 8 + 8))
        if i == 0:
            plane_self(g_out, g_in, 4)
    pltpu.make_async_copy(g_in, g_in, recv.at[4]).wait()

    for w0 in range(2):
        for w2 in range(2):
            at = w0 * 16 + w2 * 8
            a, b = g_in[pl.ds(at, 4)].reshape(32, 128), g_in[pl.ds(at + 4, 4)].reshape(32, 128)
            low, high = cross(a, b, bit5, 32)
            v_out[0, w0, pl.ds(w2 * 4, 4)] = low.reshape(4, 8, 128)
            v_out[1, w0, pl.ds(w2 * 4, 4)] = high.reshape(4, 8, 128)
    for off in Z_ORDER:
        z_to = (z + off) % 16
        for w in range(2):
            pltpu.make_async_remote_copy(
                v_out.at[z_to // 8, w, :, z_to % 8], v_in.at[tile, :, sub + w], send.at[5], recv.at[5],
                device_id=dev(p, z_to), device_id_type=MESH,
            ).start()
    for w in range(2):
        pltpu.make_async_copy(v_out.at[zh, w, :, zl], v_in.at[tile, :, sub + w], recv.at[5]).start()
    pltpu.make_async_copy(df_mid, df_mid, recv.at[8]).wait()
    spread_plane(((df_mid, dfilt),), 9)
    pltpu.make_async_copy(v_in, v_in, recv.at[5]).wait()

    for t in range(4):
        a = [pair_swap(v_in[:, w2 * 4 + t].reshape(32, 128)) for w2 in range(2)]
        re, im = cross(a[0], a[1], bit6, 64)
        outs[0, :, pl.ds(t * 128, 128)] = re
        outs[1, :, pl.ds(t * 128, 128)] = im

    pltpu.make_async_copy(dfilt, dfilt, recv.at[9]).wait()
    outs[2:] = dfilt[...].reshape(2, 32, 512)

    def sent(ref, stage):
        pltpu.make_async_copy(ref, ref, send.at[stage]).wait()

    sent(z_in.at[pl.ds(0, 30)], 0)
    sent(p_in.at[pl.ds(0, 31)], 1)
    sent(k_in.at[pl.ds(0, 31)], 2)
    sent(m_in.at[pl.ds(0, 31)], 3)
    sent(g_in.at[pl.ds(0, 31)], 4)
    sent(g_in.at[pl.ds(0, 30)], 5)
    for stage in (6, 7, 8, 9):
        sent(p_in.at[pl.ds(0, 14)], stage)


def per_device(x_re, x_im, gate_in, cot_re, cot_im, filt_re, filt_im):
    first, mid, last = (jnp.asarray(t) for t in tables())
    vm = pltpu.VMEM
    outs = pl.pallas_call(
        kernel,
        out_shape=jax.ShapeDtypeStruct((4, 32, 512), F32),
        in_specs=[pl.BlockSpec(memory_space=pl.ANY)] * 10,
        out_specs=pl.BlockSpec(memory_space=pltpu.VMEM),
        scratch_shapes=[
            vm((32, 512), F32), vm((32, 512), F32), vm((32, 512), F32), vm((32, 512), F32), vm((32, 512), F32),
            vm((2, 1024, 512), BF16), vm((2, 512, 1024), BF16), vm((2, 1024, 512), BF16),
            vm((512, 128), F32), vm((512, 128), F32), vm((32, 512), F32), vm((32, 512), F32),
            vm((4, 16, 8, 128), F32), vm((32, 16, 128), F32), vm((32, 16, 128), F32), vm((512, 256), BF16),
            vm((32, 16, 128), F32), vm((32, 16, 128), F32), vm((256, 512), BF16),
            vm((2, 2, 16, 512), F32), vm((2, 2, 16, 512), F32), vm((2, 2, 16, 512), F32), vm((2, 2, 16, 512), F32), vm((128, 512), BF16),
            vm((32, 8, 128), F32), vm((32, 8, 128), F32), vm((512, 256), BF16),
            vm((32, 8, 128), F32), vm((32, 8, 128), F32), vm((2, 2, 8, 8, 128), F32), vm((4, 8, 8, 128), F32), vm((2, 2, 16, 512), F32),
            pltpu.SemaphoreType.DMA((5,)), pltpu.SemaphoreType.DMA((3,)),
            pltpu.SemaphoreType.DMA((10,)), pltpu.SemaphoreType.DMA((10,)),
        ],
        name="spectral_backward",
        compiler_params=pltpu.CompilerParams(
            collective_id=0, has_side_effects=True, vmem_limit_bytes=60 * 1024 * 1024
        ),
    )(x_re, x_im, gate_in, cot_re, cot_im, filt_re, filt_im, first, mid, last)
    dx_re = gate_in * outs[0]
    dx_im = gate_in * outs[1]
    dgate = x_re * outs[0] + x_im * outs[1]
    dfilt_re = (outs[2] * 0.25).reshape(filt_re.shape)
    dfilt_im = (outs[3] * 0.25).reshape(filt_im.shape)
    return dx_re, dx_im, dgate, dfilt_re, dfilt_im


def solution(mesh):
    seq_in = P(None, ("grp", "seq"))
    filt = P("grp", "seq", None)
    return jax.shard_map(
        per_device,
        mesh=mesh,
        in_specs=(seq_in,) * 5 + (filt,) * 2,
        out_specs=(seq_in,) * 3 + (filt,) * 2,
        check_vma=False,
    )
```

```python
import functools
import math

import jax
import jax.numpy as jnp
import ml_dtypes
import numpy as np
from jax import lax
from jax.experimental import pallas as pl
from jax.experimental.pallas import tpu as pltpu
from jax.sharding import PartitionSpec as P

N1 = 512
N2 = 512
SEQ = N1 * N2
F32 = jnp.float32
BF16 = jnp.bfloat16
MESH = pl.DeviceIdType.MESH
Z_ORDER = (8, 7, 9, 6, 10, 5, 11, 4, 12, 3, 13, 2, 14, 1, 15)


def split_np(table):
    hi = table.astype(ml_dtypes.bfloat16)
    lo = (table - hi.astype(np.float64)).astype(ml_dtypes.bfloat16)
    return np.stack([hi, lo])


def n_of(p, z):
    return ((p % 16) // 4) * 128 + (z // 8) * 64 + (p // 16) * 32 + (p % 4) * 8 + z % 8


def k1_of(q, r):
    return (q % 4) * 128 + (r // 4) * 16 + (q // 4) * 4 + r % 4


def tables():
    idx = np.arange(512)
    n_rows = n_of(idx // 16, idx % 16)
    n_cols = n_of((idx % 256) // 8, (idx % 8) * 2 + idx // 256)
    k_rows = k1_of(idx // 32, idx % 32)
    k_cols = k1_of((idx % 256) // 16, (idx // 256) * 16 + idx % 16)

    def pair(rows, cols, factor):
        angle = (rows[:, None] * cols[None, :] % 512) * (2.0 * math.pi / 512)
        return np.cos(angle) * factor, np.sin(angle) * factor

    unit = 1.0 / math.sqrt(512.0)

    def by_rows(rows, cols, factor):
        c, s = pair(rows, cols, factor)
        return split_np(np.stack([c.reshape(4, 128, 512), s.reshape(4, 128, 512)], 1).reshape(1024, 512))

    first = by_rows(k_rows, n_cols, 2.0 * unit)
    last = by_rows(n_rows, k_cols, 0.5 * unit)
    c, s = pair(idx, idx, unit)
    mid = split_np(np.stack([c.reshape(512, 4, 128), s.reshape(512, 4, 128)], 2).reshape(512, 1024))
    return first, mid, last


def cross(first, second, bit, size):
    low = jnp.where(bit, pltpu.roll(second, size, 1), first)
    high = jnp.where(bit, second, pltpu.roll(first, 128 - size, 1))
    return low, high


def split(value):
    hi = value.astype(BF16)
    return hi, (value - hi.astype(F32)).astype(BF16)


def dot(a, b):
    return jnp.dot(a, b, preferred_element_type=F32)


def kernel(
    x_re, x_im, gate, cot_re, cot_im, filt_re, filt_im, first_hbm, mid_hbm, last_hbm,
    outs,
    vx_re, vx_im, vgate, vcot_re, vcot_im, first, mid, last, tw_cos, tw_sin, bend_cos, bend_sin,
    z_out, z_in, p_in, part, xx, k_out, k_in, dd, f_mid, f_in, df_out, df_mid, ee, m_out, m_in, xx2, g_out, g_in, v_out, v_in, dfilt,
    in_sem, tab_sem, send, recv,
):
    grp = lax.axis_index("grp")
    seq = lax.axis_index("seq")
    x, zh, c = grp // 4, (grp // 2) % 2, grp % 2
    y, zl = seq // 8, seq % 8
    z = zh * 8 + zl
    xc = x * 2 + c
    q = x * 4 + y
    p = c * 16 + q
    near = z % 2
    far = 1 - near

    def dev(p_to, z_to):
        return (((p_to // 4) % 4) * 4 + (z_to // 8) * 2 + p_to // 16, (p_to % 4) * 8 + z_to % 8)

    bar = pltpu.get_barrier_semaphore()

    def greet(p_to, z_to):
        pl.semaphore_signal(bar, inc=1, device_id=dev(p_to, z_to), device_id_type=MESH)

    loads = [
        pltpu.make_async_copy(src, dst, in_sem.at[i])
        for i, (src, dst) in enumerate(
            ((x_re, vx_re), (x_im, vx_im), (gate, vgate), (cot_re, vcot_re), (cot_im, vcot_im))
        )
    ]
    for load in loads:
        load.start()
    for off in Z_ORDER:
        greet(p, (z + off) % 16)
    for off in range(31, 0, -1):
        greet(p ^ off, z)
    table_loads = [
        pltpu.make_async_copy(src, dst, tab_sem.at[i])
        for i, (src, dst) in enumerate(((first_hbm, first), (mid_hbm, mid), (last_hbm, last)))
    ]
    for load in table_loads:
        load.start()

    lane = lax.broadcasted_iota(jnp.int32, (32, 128), 1)
    row = lax.broadcasted_iota(jnp.int32, (32, 128), 0)
    bit6 = (lane & 64) != 0
    bit5 = (lane & 32) != 0

    for load in loads:
        load.wait()
    for t in range(4):
        cols = pl.ds(t * 128, 128)
        g = vgate[:, cols]
        a = [vx_re[:, cols] * g, vcot_re[:, cols], vx_im[:, cols] * g, vcot_im[:, cols]]
        b = [None] * 4
        b[0], b[2] = cross(a[0], a[2], bit6, 64)
        b[1], b[3] = cross(a[1], a[3], bit6, 64)
        w = [None] * 4
        w[0], w[1] = cross(b[0], b[1], bit5, 32)
        w[2], w[3] = cross(b[2], b[3], bit5, 32)
        for i in range(4):
            z_out[:, i * 4 + t] = w[i].reshape(4, 8, 128)

    pl.semaphore_wait(bar, 46)

    def z_rows(z_to):
        return (z_to % 8) // 2, (z_to // 8) * 4 + (z_to % 2) * 2

    for off in Z_ORDER:
        stage = 0 if off % 2 else 10
        z_to = (z + off) % 16
        tile, sub = z_rows(z_to)
        for l in range(2):
            pltpu.make_async_remote_copy(
                z_out.at[tile, :, sub + l], z_in.at[near, pl.ds(l * 16, 16), z // 2],
                send.at[stage], recv.at[stage], device_id=dev(p, z_to), device_id_type=MESH,
            ).start()
    tile, sub = z_rows(z)
    for l in range(2):
        pltpu.make_async_copy(z_out.at[tile, :, sub + l], z_in.at[near, pl.ds(l * 16, 16), z // 2], recv.at[10]).start()

    def own_rows(k):
        return pl.ds(4 * k, 4)

    def plane_step(stage, moves):
        for off in (7, 5, 3, 6, 4, 2, 1, 0):
            other = xc ^ off
            for src, dst in moves(other // 2, other % 2, other):
                if off:
                    pltpu.make_async_remote_copy(
                        src, dst, send.at[stage], recv.at[stage],
                        device_id=dev((other % 2) * 16 + (other // 2) * 4 + y, z), device_id_type=MESH,
                    ).start()
                else:
                    pltpu.make_async_copy(src, dst, recv.at[stage]).start()

    def line_step(src, dst, stage):
        for off in range(7, 0, -1):
            pltpu.make_async_remote_copy(
                src.at[:, own_rows(zl ^ off), :], dst.at[:, own_rows(zl), :],
                send.at[stage], recv.at[stage], device_id=dev(p, z ^ off), device_id_type=MESH,
            ).start()
        pltpu.make_async_copy(src.at[:, own_rows(zl), :], dst.at[:, own_rows(zl), :], recv.at[stage]).start()

    plane_step(
        6,
        lambda x_to, c_to, xc_to: (
            (filt_re.at[c_to, own_rows(x_to), :], f_mid.at[0, own_rows(xc), :]),
            (filt_im.at[c_to, own_rows(x_to), :], f_mid.at[1, own_rows(xc), :]),
        ),
    )

    def angles(k, m):
        return (k * m).astype(F32) * (2.0 * math.pi / SEQ)

    sign = jnp.where(lax.broadcasted_iota(jnp.int32, (128, 128), 1) < 64, 1.0, -1.0).astype(F32)
    m_lane = lax.broadcasted_iota(jnp.int32, (128, 128), 1) % 32 + (y * 128 + x * 32)
    for i in range(4):
        k_row = lax.broadcasted_iota(jnp.int32, (128, 128), 0) + i * 128
        theta = angles(k1_of(k_row // 32, k_row % 32), m_lane)
        tw_cos[pl.ds(i * 128, 128), :] = jnp.cos(theta)
        tw_sin[pl.ds(i * 128, 128), :] = jnp.sin(theta) * sign
        theta = angles(k1_of(q, row), lane + i * 128)
        bend_cos[:, pl.ds(i * 128, 128)] = jnp.cos(theta)
        bend_sin[:, pl.ds(i * 128, 128)] = jnp.sin(theta)

    def plane(src, dst, stage, offs, own):
        for off in offs:
            pltpu.make_async_remote_copy(
                src.at[p ^ off], dst.at[p], send.at[stage], recv.at[stage],
                device_id=dev(p ^ off, z), device_id_type=MESH,
            ).start()
        if own:
            pltpu.make_async_copy(src.at[p], dst.at[p], recv.at[stage]).start()

    def chips(src, dst, stage, offs, own):
        for off in offs:
            pltpu.make_async_remote_copy(
                src.at[q ^ off], dst.at[q], send.at[stage], recv.at[stage],
                device_id=dev(p ^ off, z), device_id_type=MESH,
            ).start()
        if own:
            pltpu.make_async_copy(src.at[q], dst.at[q], recv.at[stage]).start()

    halves = ((far, 0, 1), (near, 10, 11))
    for half, got, stage in halves:
        pltpu.make_async_copy(z_in.at[half], z_in.at[half], recv.at[got]).wait()
        plane(z_in.at[half], p_in.at[half], stage, range(31, 0, -1), True)
    pltpu.make_async_copy(f_mid, f_mid, recv.at[6]).wait()
    line_step(f_mid, f_in, 7)

    table_loads[0].wait()
    for at, (half, got, stage) in enumerate(halves):
        pltpu.make_async_copy(p_in.at[half], p_in.at[half], recv.at[stage]).wait()
        hi, lo = split(p_in[half].reshape(256, 128))
        xx[at, :, :128] = hi
        xx[at, :, 128:] = lo
        depth = pl.ds(pl.multiple_of(half * 256, 256), 256)
        for i in range(4):
            chunk = (q // 4) ^ i
            rows = pl.ds(pl.multiple_of(chunk * 256, 256), 256)
            out = dot(first[0, rows, depth], xx[at]) + dot(first[1, rows, depth], xx[at])
            acc = out[:, :128] + out[:, 128:]
            if at == 0:
                part[i] = acc
                continue
            acc = acc + part[i]
            spec = acc[:128] + sign * pltpu.roll(acc[128:], 64, 1)
            rows = pl.ds(pl.multiple_of(chunk * 128, 128), 128)
            turned = spec * tw_cos[rows, :] + pltpu.roll(spec, 64, 1) * tw_sin[rows, :]
            k_out[pl.ds(chunk * 4, 4)] = turned.reshape(4, 32, 128)
            chips(k_out, k_in, 2, range(i * 4 + (i == 0), i * 4 + 4), i == 0)

    table_loads[1].wait()
    pltpu.make_async_copy(k_in, k_in, recv.at[2]).wait()

    for t in range(4):
        cols = pl.ds(t * 128, 128)
        a = [cross(k_in[w1 * 4 + t], k_in[8 + w1 * 4 + t], bit6, 64) for w1 in range(2)]
        for ri in range(2):
            b = cross(a[0][ri], a[1][ri], bit5, 32)
            for ug in range(2):
                hi, lo = split(b[ug])
                dd[pl.ds(ri * 64 + ug * 32, 32), cols] = hi
                dd[pl.ds(128 + ri * 64 + ug * 32, 32), cols] = lo

    pltpu.make_async_copy(f_in, f_in, recv.at[7]).wait()
    for i in range(4):
        wide = pl.ds(i * 256, 256)
        cols = pl.ds(i * 128, 128)
        out = dot(dd[...], mid[0, :, wide]) + dot(dd[...], mid[1, :, wide])
        acc = out[:128] + out[128:]
        re = acc[:64, :128] + acc[64:, 128:]
        im = acc[64:, :128] - acc[:64, 128:]
        u_re, g_re, u_im, g_im = re[:32], re[32:], im[:32], im[32:]
        df_out[0, :, cols] = g_re * u_re + g_im * u_im
        df_out[1, :, cols] = g_im * u_re - g_re * u_im
        f_re = f_in[0, :, cols]
        f_im = f_in[1, :, cols]
        hi, lo = split(jnp.concatenate([f_re * g_re + f_im * g_im, f_re * g_im - f_im * g_re], 0))
        ee[:64, cols] = hi
        ee[64:, cols] = lo
    line_step(df_out, df_mid, 8)

    mask5 = bit5[:16]
    for t in range(4):
        wide = pl.ds(t * 256, 256)
        cols = pl.ds(t * 128, 128)
        out = dot(ee[...], mid[0, :, wide]) + dot(ee[...], mid[1, :, wide])
        acc = out[:64] + out[64:]
        re = acc[:32, :128] - acc[32:, 128:]
        im = acc[32:, :128] + acc[:32, 128:]
        b_cos, b_sin = bend_cos[:, cols], bend_sin[:, cols]
        bent = cross(re * b_cos - im * b_sin, im * b_cos + re * b_sin, bit6, 64)
        for w2 in range(2):
            d = cross(bent[w2][:16], bent[w2][16:], mask5, 32)
            for w1 in range(2):
                m_out[w2 * 8 + w1 * 4 + t] = d[w1]

    chips(m_out, m_in, 3, range(15, 0, -1), True)

    table_loads[2].wait()
    pltpu.make_async_copy(m_in, m_in, recv.at[3]).wait()

    v = m_in[...].reshape(256, 128)
    wide5 = (lax.broadcasted_iota(jnp.int32, (256, 128), 1) & 32) != 0
    hi, lo = split(jnp.where(wide5, pltpu.roll(v, 32, 1), v))
    xx2[:256, :128] = hi
    xx2[:256, 128:] = lo
    hi, lo = split(jnp.where(wide5, v, pltpu.roll(v, 96, 1)))
    xx2[256:, :128] = hi
    xx2[256:, 128:] = lo
    pick5 = (lax.broadcasted_iota(jnp.int32, (8, 8, 128), 2) & 32) != 0
    for i in range(4):
        chunk = (p // 8) ^ i
        rows = pl.ds(pl.multiple_of(chunk * 256, 256), 256)
        out = dot(last[0, rows, :], xx2[...]) + dot(last[1, rows, :], xx2[...])
        acc = out[:, :128] + out[:, 128:]
        g = (acc[:128] - sign * pltpu.roll(acc[128:], 64, 1)).reshape(8, 2, 8, 128)
        g_out[pl.ds(chunk * 8, 8)] = jnp.where(pick5, g[:, 1], g[:, 0])
        plane(g_out, g_in, 4, range(i * 8 + (i == 0), i * 8 + 8), i == 0)
    pltpu.make_async_copy(g_in, g_in, recv.at[4]).wait()

    for l in range(2):
        for w2 in range(2):
            at = l * 16 + w2 * 8
            a, b = g_in[pl.ds(at, 4)].reshape(32, 128), g_in[pl.ds(at + 4, 4)].reshape(32, 128)
            low, high = cross(a, b, bit5, 32)
            v_out[0, l, pl.ds(w2 * 4, 4)] = low.reshape(4, 8, 128)
            v_out[1, l, pl.ds(w2 * 4, 4)] = high.reshape(4, 8, 128)
    for off in Z_ORDER:
        z_to = (z + off) % 16
        for l in range(2):
            pltpu.make_async_remote_copy(
                v_out.at[z_to // 8, l, :, z_to % 8], v_in.at[tile, :, sub + l], send.at[5], recv.at[5],
                device_id=dev(p, z_to), device_id_type=MESH,
            ).start()
    for l in range(2):
        pltpu.make_async_copy(v_out.at[zh, l, :, zl], v_in.at[tile, :, sub + l], recv.at[5]).start()
    pltpu.make_async_copy(df_mid, df_mid, recv.at[8]).wait()
    plane_step(
        9, lambda x_to, c_to, xc_to: ((df_mid.at[:, own_rows(xc_to), :], dfilt.at[:, c, own_rows(x), :]),)
    )
    pltpu.make_async_copy(v_in, v_in, recv.at[5]).wait()

    for t in range(4):
        a = [v_in[:, w2 * 4 + t].reshape(32, 128) for w2 in range(2)]
        re, im = cross(a[0], a[1], bit6, 64)
        outs[0, :, pl.ds(t * 128, 128)] = re
        outs[1, :, pl.ds(t * 128, 128)] = im

    pltpu.make_async_copy(dfilt, dfilt, recv.at[9]).wait()
    outs[2:] = dfilt[...].reshape(2, 32, 512)

    def sent(ref, stage):
        pltpu.make_async_copy(ref, ref, send.at[stage]).wait()

    sent(z_in.at[0], 0)
    sent(z_in.at[0, pl.ds(0, 28)], 10)
    for stage in (1, 11):
        sent(z_in.at[0, pl.ds(0, 31)], stage)
    sent(k_in.at[pl.ds(0, 15)], 2)
    sent(m_in.at[pl.ds(0, 15)], 3)
    sent(g_in.at[pl.ds(0, 31)], 4)
    sent(g_in.at[pl.ds(0, 30)], 5)
    for stage in (6, 7, 8, 9):
        sent(m_in.at[pl.ds(0, 14)], stage)


def finish(x_re, x_im, gate, outs, dx_re, dx_im, dgate, dfilt_re, dfilt_im):
    dx_re[...] = gate[...] * outs[0]
    dx_im[...] = gate[...] * outs[1]
    dgate[...] = x_re[...] * outs[0] + x_im[...] * outs[1]
    dfilt_re[...] = (outs[2] * 0.25).reshape(2, 16, 512)
    dfilt_im[...] = (outs[3] * 0.25).reshape(2, 16, 512)


def per_device(x_re, x_im, gate_in, cot_re, cot_im, filt_re, filt_im):
    first, mid, last = (jnp.asarray(t) for t in tables())
    vm = pltpu.VMEM
    outs = pl.pallas_call(
        kernel,
        out_shape=jax.ShapeDtypeStruct((4, 32, 512), F32),
        in_specs=[pl.BlockSpec(memory_space=pl.ANY)] * 10,
        out_specs=pl.BlockSpec(memory_space=pltpu.VMEM),
        scratch_shapes=[
            vm((32, 512), F32), vm((32, 512), F32), vm((32, 512), F32), vm((32, 512), F32), vm((32, 512), F32),
            vm((2, 1024, 512), BF16), vm((2, 512, 1024), BF16), vm((2, 1024, 512), BF16),
            vm((512, 128), F32), vm((512, 128), F32), vm((32, 512), F32), vm((32, 512), F32),
            vm((4, 16, 8, 128), F32), vm((2, 32, 8, 128), F32), vm((2, 32, 8, 128), F32), vm((4, 256, 128), F32),
            vm((2, 256, 256), BF16), vm((16, 32, 128), F32), vm((16, 32, 128), F32), vm((256, 512), BF16),
            vm((2, 32, 512), F32), vm((2, 32, 512), F32), vm((2, 32, 512), F32), vm((2, 32, 512), F32),
            vm((128, 512), BF16), vm((16, 16, 128), F32), vm((16, 16, 128), F32), vm((512, 256), BF16),
            vm((32, 8, 128), F32), vm((32, 8, 128), F32), vm((2, 2, 8, 8, 128), F32), vm((4, 8, 8, 128), F32),
            vm((2, 2, 16, 512), F32),
            pltpu.SemaphoreType.DMA((5,)), pltpu.SemaphoreType.DMA((3,)),
            pltpu.SemaphoreType.DMA((12,)), pltpu.SemaphoreType.DMA((12,)),
        ],
        name="spectral_backward",
        compiler_params=pltpu.CompilerParams(
            collective_id=0, has_side_effects=True, vmem_limit_bytes=60 * 1024 * 1024
        ),
    )(x_re, x_im, gate_in, cot_re, cot_im, filt_re, filt_im, first, mid, last)
    vmem = pl.BlockSpec(memory_space=pltpu.VMEM)
    wide = jax.ShapeDtypeStruct((32, 512), F32)
    return pl.pallas_call(
        finish,
        out_shape=(wide, wide, wide) + (jax.ShapeDtypeStruct(filt_re.shape, F32),) * 2,
        in_specs=[vmem] * 4,
        out_specs=(vmem,) * 5,
        name="products",
    )(x_re, x_im, gate_in, outs)


def solution(mesh):
    seq_in = P(None, ("grp", "seq"))
    filt = P("grp", "seq", None)
    return jax.shard_map(
        per_device,
        mesh=mesh,
        in_specs=(seq_in,) * 5 + (filt,) * 2,
        out_specs=(seq_in,) * 3 + (filt,) * 2,
        check_vma=False,
    )
```

```python
import functools
import math

import jax
import jax.numpy as jnp
import ml_dtypes
import numpy as np
from jax import lax
from jax.experimental import pallas as pl
from jax.experimental.pallas import tpu as pltpu
from jax.sharding import PartitionSpec as P

N1 = 512
N2 = 512
SEQ = N1 * N2
F32 = jnp.float32
BF16 = jnp.bfloat16
MESH = pl.DeviceIdType.MESH
Z_ORDER = (8, 7, 9, 6, 10, 5, 11, 4, 12, 3, 13, 2, 14, 1, 15)


def split_np(table):
    hi = table.astype(ml_dtypes.bfloat16)
    lo = (table - hi.astype(np.float64)).astype(ml_dtypes.bfloat16)
    return np.stack([hi, lo])


def n_of(p, z):
    return ((p % 16) // 4) * 128 + (z // 8) * 64 + (p // 16) * 32 + (p % 4) * 8 + z % 8


def k1_of(q, r):
    return (q % 4) * 128 + (r // 4) * 16 + (q // 4) * 4 + r % 4


def tables():
    idx = np.arange(512)
    n_rows = n_of(idx // 16, idx % 16)
    n_cols = n_of((idx % 256) // 8, (idx % 8) * 2 + idx // 256)
    k_rows = k1_of(idx // 32, idx % 32)
    k_cols = k1_of((idx % 256) // 16, (idx // 256) * 16 + idx % 16)

    def pair(rows, cols, factor):
        angle = (rows[:, None] * cols[None, :] % 512) * (2.0 * math.pi / 512)
        return np.cos(angle) * factor, np.sin(angle) * factor

    unit = 1.0 / math.sqrt(512.0)

    def by_rows(rows, cols, factor):
        c, s = pair(rows, cols, factor)
        return split_np(np.stack([c.reshape(4, 128, 512), s.reshape(4, 128, 512)], 1).reshape(1024, 512))

    first = by_rows(k_rows, n_cols, 2.0 * unit)
    last = by_rows(n_rows, k_cols, 0.5 * unit)
    c, s = pair(idx, idx, unit)
    mid = split_np(np.stack([c.reshape(512, 4, 128), s.reshape(512, 4, 128)], 2).reshape(512, 1024))
    return first, mid, last


def cross(first, second, bit, size):
    low = jnp.where(bit, pltpu.roll(second, size, 1), first)
    high = jnp.where(bit, second, pltpu.roll(first, 128 - size, 1))
    return low, high


def split(value):
    hi = value.astype(BF16)
    return hi, (value - hi.astype(F32)).astype(BF16)


def dot(a, b):
    return jnp.dot(a, b, preferred_element_type=F32)


def kernel(
    x_re, x_im, gate, cot_re, cot_im, filt_re, filt_im, first_hbm, mid_hbm, last_hbm,
    outs,
    vx_re, vx_im, vgate, vcot_re, vcot_im, first, mid, last, tw_cos, tw_sin, bend_cos, bend_sin,
    z_out, z_in, p_in, part, xx, k_out, k_in, dd, g_keep, f_mid, f_in, df_out, df_mid, ee, m_out, m_in, xx2, g_out, g_in, v_out, v_in, dfilt,
    in_sem, tab_sem, send, recv,
):
    grp = lax.axis_index("grp")
    seq = lax.axis_index("seq")
    x, zh, c = grp // 4, (grp // 2) % 2, grp % 2
    y, zl = seq // 8, seq % 8
    z = zh * 8 + zl
    xc = x * 2 + c
    q = x * 4 + y
    p = c * 16 + q
    near = z % 2
    far = 1 - near

    def dev(p_to, z_to):
        return (((p_to // 4) % 4) * 4 + (z_to // 8) * 2 + p_to // 16, (p_to % 4) * 8 + z_to % 8)

    bar = pltpu.get_barrier_semaphore()

    def greet(p_to, z_to):
        pl.semaphore_signal(bar, inc=1, device_id=dev(p_to, z_to), device_id_type=MESH)

    loads = [
        pltpu.make_async_copy(src, dst, in_sem.at[i])
        for i, (src, dst) in enumerate(
            ((x_re, vx_re), (x_im, vx_im), (gate, vgate), (cot_re, vcot_re), (cot_im, vcot_im))
        )
    ]
    for load in loads:
        load.start()
    for off in Z_ORDER:
        greet(p, (z + off) % 16)
    for off in range(31, 0, -1):
        greet(p ^ off, z)
    table_loads = [
        pltpu.make_async_copy(src, dst, tab_sem.at[i])
        for i, (src, dst) in enumerate(((first_hbm, first), (mid_hbm, mid), (last_hbm, last)))
    ]
    for load in table_loads:
        load.start()

    lane = lax.broadcasted_iota(jnp.int32, (32, 128), 1)
    row = lax.broadcasted_iota(jnp.int32, (32, 128), 0)
    bit6 = (lane & 64) != 0
    bit5 = (lane & 32) != 0

    for load in loads:
        load.wait()
    for t in range(4):
        cols = pl.ds(t * 128, 128)
        g = vgate[:, cols]
        a = [vx_re[:, cols] * g, vcot_re[:, cols], vx_im[:, cols] * g, vcot_im[:, cols]]
        b = [None] * 4
        b[0], b[2] = cross(a[0], a[2], bit6, 64)
        b[1], b[3] = cross(a[1], a[3], bit6, 64)
        w = [None] * 4
        w[0], w[1] = cross(b[0], b[1], bit5, 32)
        w[2], w[3] = cross(b[2], b[3], bit5, 32)
        for i in range(4):
            z_out[:, i * 4 + t] = w[i].reshape(4, 8, 128)

    pl.semaphore_wait(bar, 46)

    def z_rows(z_to):
        return (z_to % 8) // 2, (z_to // 8) * 4 + (z_to % 2) * 2

    for off in Z_ORDER:
        stage = 0 if off % 2 else 10
        z_to = (z + off) % 16
        tile, sub = z_rows(z_to)
        for l in range(2):
            pltpu.make_async_remote_copy(
                z_out.at[tile, :, sub + l], z_in.at[near, pl.ds(l * 16, 16), z // 2],
                send.at[stage], recv.at[stage], device_id=dev(p, z_to), device_id_type=MESH,
            ).start()
    tile, sub = z_rows(z)
    for l in range(2):
        pltpu.make_async_copy(z_out.at[tile, :, sub + l], z_in.at[near, pl.ds(l * 16, 16), z // 2], recv.at[10]).start()

    def own_rows(k):
        return pl.ds(4 * k, 4)

    def plane_step(stage, moves):
        for off in (7, 5, 3, 6, 4, 2, 1, 0):
            other = xc ^ off
            for src, dst in moves(other // 2, other % 2, other):
                if off:
                    pltpu.make_async_remote_copy(
                        src, dst, send.at[stage], recv.at[stage],
                        device_id=dev((other % 2) * 16 + (other // 2) * 4 + y, z), device_id_type=MESH,
                    ).start()
                else:
                    pltpu.make_async_copy(src, dst, recv.at[stage]).start()

    def line_step(src, dst, stage):
        for off in range(7, 0, -1):
            pltpu.make_async_remote_copy(
                src.at[:, own_rows(zl ^ off), :], dst.at[:, own_rows(zl), :],
                send.at[stage], recv.at[stage], device_id=dev(p, z ^ off), device_id_type=MESH,
            ).start()
        pltpu.make_async_copy(src.at[:, own_rows(zl), :], dst.at[:, own_rows(zl), :], recv.at[stage]).start()

    plane_step(
        6,
        lambda x_to, c_to, xc_to: (
            (filt_re.at[c_to, own_rows(x_to), :], f_mid.at[0, own_rows(xc), :]),
            (filt_im.at[c_to, own_rows(x_to), :], f_mid.at[1, own_rows(xc), :]),
        ),
    )

    def angles(k, m):
        return (k * m).astype(F32) * (2.0 * math.pi / SEQ)

    sign = jnp.where(lax.broadcasted_iota(jnp.int32, (128, 128), 1) < 64, 1.0, -1.0).astype(F32)
    m_lane = lax.broadcasted_iota(jnp.int32, (128, 128), 1) % 32 + (y * 128 + x * 32)
    for i in range(4):
        k_row = lax.broadcasted_iota(jnp.int32, (128, 128), 0) + i * 128
        theta = angles(k1_of(k_row // 32, k_row % 32), m_lane)
        tw_cos[pl.ds(i * 128, 128), :] = jnp.cos(theta)
        tw_sin[pl.ds(i * 128, 128), :] = jnp.sin(theta) * sign
        theta = angles(k1_of(q, row), lane + i * 128)
        bend_cos[:, pl.ds(i * 128, 128)] = jnp.cos(theta)
        bend_sin[:, pl.ds(i * 128, 128)] = jnp.sin(theta)

    def plane(src, dst, stage, offs, own):
        for off in offs:
            pltpu.make_async_remote_copy(
                src.at[p ^ off], dst.at[p], send.at[stage], recv.at[stage],
                device_id=dev(p ^ off, z), device_id_type=MESH,
            ).start()
        if own:
            pltpu.make_async_copy(src.at[p], dst.at[p], recv.at[stage]).start()

    def chips(src, dst, stage, offs, own):
        for off in offs:
            pltpu.make_async_remote_copy(
                src.at[q ^ off], dst.at[q], send.at[stage], recv.at[stage],
                device_id=dev(p ^ off, z), device_id_type=MESH,
            ).start()
        if own:
            pltpu.make_async_copy(src.at[q], dst.at[q], recv.at[stage]).start()

    halves = ((far, 0, 1), (near, 10, 11))
    for half, got, stage in halves:
        pltpu.make_async_copy(z_in.at[half], z_in.at[half], recv.at[got]).wait()
        plane(z_in.at[half], p_in.at[half], stage, range(31, 0, -1), True)
    pltpu.make_async_copy(f_mid, f_mid, recv.at[6]).wait()
    line_step(f_mid, f_in, 7)

    table_loads[0].wait()
    for at, (half, got, stage) in enumerate(halves):
        pltpu.make_async_copy(p_in.at[half], p_in.at[half], recv.at[stage]).wait()
        hi, lo = split(p_in[half].reshape(256, 128))
        xx[at, :, :128] = hi
        xx[at, :, 128:] = lo
        depth = pl.ds(pl.multiple_of(half * 256, 256), 256)
        for i in range(4):
            chunk = (q // 4) ^ i
            rows = pl.ds(pl.multiple_of(chunk * 256, 256), 256)
            out = dot(first[0, rows, depth], xx[at]) + dot(first[1, rows, depth], xx[at])
            acc = out[:, :128] + out[:, 128:]
            if at == 0:
                part[i] = acc
                continue
            acc = acc + part[i]
            spec = acc[:128] + sign * pltpu.roll(acc[128:], 64, 1)
            rows = pl.ds(pl.multiple_of(chunk * 128, 128), 128)
            turned = spec * tw_cos[rows, :] + pltpu.roll(spec, 64, 1) * tw_sin[rows, :]
            k_out[pl.ds(chunk * 4, 4)] = turned.reshape(4, 32, 128)
            chips(k_out, k_in, 2, range(i * 4 + (i == 0), i * 4 + 4), i == 0)

    table_loads[1].wait()
    pltpu.make_async_copy(k_in, k_in, recv.at[2]).wait()

    for t in range(4):
        cols = pl.ds(t * 128, 128)
        a = [cross(k_in[w1 * 4 + t], k_in[8 + w1 * 4 + t], bit6, 64) for w1 in range(2)]
        for ri in range(2):
            b = cross(a[0][ri], a[1][ri], bit5, 32)
            for ug in range(2):
                hi, lo = split(b[ug])
                dd[ug, pl.ds(ri * 32, 32), cols] = hi
                dd[ug, pl.ds(64 + ri * 32, 32), cols] = lo

    def spectrum(which, i):
        wide = pl.ds(i * 256, 256)
        out = dot(dd[which], mid[0, :, wide]) + dot(dd[which], mid[1, :, wide])
        acc = out[:64] + out[64:]
        return acc[:32, :128] + acc[32:, 128:], acc[32:, :128] - acc[:32, 128:]

    pltpu.make_async_copy(f_in, f_in, recv.at[7]).wait()
    for i in range(4):
        cols = pl.ds(i * 128, 128)
        g_re, g_im = spectrum(1, i)
        g_keep[0, :, cols] = g_re
        g_keep[1, :, cols] = g_im
        f_re = f_in[0, :, cols]
        f_im = f_in[1, :, cols]
        hi, lo = split(jnp.concatenate([f_re * g_re + f_im * g_im, f_re * g_im - f_im * g_re], 0))
        ee[:64, cols] = hi
        ee[64:, cols] = lo

    mask5 = bit5[:16]
    for t in range(4):
        wide = pl.ds(t * 256, 256)
        cols = pl.ds(t * 128, 128)
        out = dot(ee[...], mid[0, :, wide]) + dot(ee[...], mid[1, :, wide])
        acc = out[:64] + out[64:]
        re = acc[:32, :128] - acc[32:, 128:]
        im = acc[32:, :128] + acc[:32, 128:]
        b_cos, b_sin = bend_cos[:, cols], bend_sin[:, cols]
        bent = cross(re * b_cos - im * b_sin, im * b_cos + re * b_sin, bit6, 64)
        for w2 in range(2):
            d = cross(bent[w2][:16], bent[w2][16:], mask5, 32)
            for w1 in range(2):
                m_out[w2 * 8 + w1 * 4 + t] = d[w1]

    chips(m_out, m_in, 3, range(15, 0, -1), True)

    for i in range(4):
        cols = pl.ds(i * 128, 128)
        u_re, u_im = spectrum(0, i)
        g_re, g_im = g_keep[0, :, cols], g_keep[1, :, cols]
        df_out[0, :, cols] = g_re * u_re + g_im * u_im
        df_out[1, :, cols] = g_im * u_re - g_re * u_im
    line_step(df_out, df_mid, 8)

    table_loads[2].wait()
    pltpu.make_async_copy(m_in, m_in, recv.at[3]).wait()

    v = m_in[...].reshape(256, 128)
    wide5 = (lax.broadcasted_iota(jnp.int32, (256, 128), 1) & 32) != 0
    hi, lo = split(jnp.where(wide5, pltpu.roll(v, 32, 1), v))
    xx2[:256, :128] = hi
    xx2[:256, 128:] = lo
    hi, lo = split(jnp.where(wide5, v, pltpu.roll(v, 96, 1)))
    xx2[256:, :128] = hi
    xx2[256:, 128:] = lo
    pick5 = (lax.broadcasted_iota(jnp.int32, (8, 8, 128), 2) & 32) != 0
    for i in range(4):
        chunk = (p // 8) ^ i
        rows = pl.ds(pl.multiple_of(chunk * 256, 256), 256)
        out = dot(last[0, rows, :], xx2[...]) + dot(last[1, rows, :], xx2[...])
        acc = out[:, :128] + out[:, 128:]
        g = (acc[:128] - sign * pltpu.roll(acc[128:], 64, 1)).reshape(8, 2, 8, 128)
        g_out[pl.ds(chunk * 8, 8)] = jnp.where(pick5, g[:, 1], g[:, 0])
        plane(g_out, g_in, 4, range(i * 8 + (i == 0), i * 8 + 8), i == 0)
    pltpu.make_async_copy(g_in, g_in, recv.at[4]).wait()

    for l in range(2):
        for w2 in range(2):
            at = l * 16 + w2 * 8
            a, b = g_in[pl.ds(at, 4)].reshape(32, 128), g_in[pl.ds(at + 4, 4)].reshape(32, 128)
            low, high = cross(a, b, bit5, 32)
            v_out[0, l, pl.ds(w2 * 4, 4)] = low.reshape(4, 8, 128)
            v_out[1, l, pl.ds(w2 * 4, 4)] = high.reshape(4, 8, 128)
    for off in Z_ORDER:
        z_to = (z + off) % 16
        for l in range(2):
            pltpu.make_async_remote_copy(
                v_out.at[z_to // 8, l, :, z_to % 8], v_in.at[tile, :, sub + l], send.at[5], recv.at[5],
                device_id=dev(p, z_to), device_id_type=MESH,
            ).start()
    for l in range(2):
        pltpu.make_async_copy(v_out.at[zh, l, :, zl], v_in.at[tile, :, sub + l], recv.at[5]).start()
    pltpu.make_async_copy(df_mid, df_mid, recv.at[8]).wait()
    plane_step(
        9, lambda x_to, c_to, xc_to: ((df_mid.at[:, own_rows(xc_to), :], dfilt.at[:, c, own_rows(x), :]),)
    )
    pltpu.make_async_copy(v_in, v_in, recv.at[5]).wait()

    for t in range(4):
        a = [v_in[:, w2 * 4 + t].reshape(32, 128) for w2 in range(2)]
        re, im = cross(a[0], a[1], bit6, 64)
        outs[0, :, pl.ds(t * 128, 128)] = re
        outs[1, :, pl.ds(t * 128, 128)] = im

    pltpu.make_async_copy(dfilt, dfilt, recv.at[9]).wait()
    outs[2:] = dfilt[...].reshape(2, 32, 512)

    def sent(ref, stage):
        pltpu.make_async_copy(ref, ref, send.at[stage]).wait()

    sent(z_in.at[0], 0)
    sent(z_in.at[0, pl.ds(0, 28)], 10)
    for stage in (1, 11):
        sent(z_in.at[0, pl.ds(0, 31)], stage)
    sent(k_in.at[pl.ds(0, 15)], 2)
    sent(m_in.at[pl.ds(0, 15)], 3)
    sent(g_in.at[pl.ds(0, 31)], 4)
    sent(g_in.at[pl.ds(0, 30)], 5)
    for stage in (6, 7, 8, 9):
        sent(m_in.at[pl.ds(0, 14)], stage)


def finish(x_re, x_im, gate, outs, dx_re, dx_im, dgate, dfilt_re, dfilt_im):
    dx_re[...] = gate[...] * outs[0]
    dx_im[...] = gate[...] * outs[1]
    dgate[...] = x_re[...] * outs[0] + x_im[...] * outs[1]
    dfilt_re[...] = (outs[2] * 0.25).reshape(2, 16, 512)
    dfilt_im[...] = (outs[3] * 0.25).reshape(2, 16, 512)


def per_device(x_re, x_im, gate_in, cot_re, cot_im, filt_re, filt_im):
    first, mid, last = (jnp.asarray(t) for t in tables())
    vm = pltpu.VMEM
    outs = pl.pallas_call(
        kernel,
        out_shape=jax.ShapeDtypeStruct((4, 32, 512), F32),
        in_specs=[pl.BlockSpec(memory_space=pl.ANY)] * 10,
        out_specs=pl.BlockSpec(memory_space=pltpu.VMEM),
        scratch_shapes=[
            vm((32, 512), F32), vm((32, 512), F32), vm((32, 512), F32), vm((32, 512), F32), vm((32, 512), F32),
            vm((2, 1024, 512), BF16), vm((2, 512, 1024), BF16), vm((2, 1024, 512), BF16),
            vm((512, 128), F32), vm((512, 128), F32), vm((32, 512), F32), vm((32, 512), F32),
            vm((4, 16, 8, 128), F32), vm((2, 32, 8, 128), F32), vm((2, 32, 8, 128), F32), vm((4, 256, 128), F32),
            vm((2, 256, 256), BF16), vm((16, 32, 128), F32), vm((16, 32, 128), F32), vm((2, 128, 512), BF16),
            vm((2, 32, 512), F32),
            vm((2, 32, 512), F32), vm((2, 32, 512), F32), vm((2, 32, 512), F32), vm((2, 32, 512), F32),
            vm((128, 512), BF16), vm((16, 16, 128), F32), vm((16, 16, 128), F32), vm((512, 256), BF16),
            vm((32, 8, 128), F32), vm((32, 8, 128), F32), vm((2, 2, 8, 8, 128), F32), vm((4, 8, 8, 128), F32),
            vm((2, 2, 16, 512), F32),
            pltpu.SemaphoreType.DMA((5,)), pltpu.SemaphoreType.DMA((3,)),
            pltpu.SemaphoreType.DMA((12,)), pltpu.SemaphoreType.DMA((12,)),
        ],
        name="spectral_backward",
        compiler_params=pltpu.CompilerParams(
            collective_id=0, has_side_effects=True, vmem_limit_bytes=60 * 1024 * 1024
        ),
    )(x_re, x_im, gate_in, cot_re, cot_im, filt_re, filt_im, first, mid, last)
    vmem = pl.BlockSpec(memory_space=pltpu.VMEM)
    wide = jax.ShapeDtypeStruct((32, 512), F32)
    return pl.pallas_call(
        finish,
        out_shape=(wide, wide, wide) + (jax.ShapeDtypeStruct(filt_re.shape, F32),) * 2,
        in_specs=[vmem] * 4,
        out_specs=(vmem,) * 5,
        name="products",
    )(x_re, x_im, gate_in, outs)


def solution(mesh):
    seq_in = P(None, ("grp", "seq"))
    filt = P("grp", "seq", None)
    return jax.shard_map(
        per_device,
        mesh=mesh,
        in_specs=(seq_in,) * 5 + (filt,) * 2,
        out_specs=(seq_in,) * 3 + (filt,) * 2,
        check_vma=False,
    )
```

```python
import functools
import math

import jax
import jax.numpy as jnp
import ml_dtypes
import numpy as np
from jax import lax
from jax.experimental import pallas as pl
from jax.experimental.pallas import tpu as pltpu
from jax.sharding import PartitionSpec as P

N1 = 512
N2 = 512
SEQ = N1 * N2
F32 = jnp.float32
BF16 = jnp.bfloat16
MESH = pl.DeviceIdType.MESH
Z_ORDER = (8, 7, 9, 6, 10, 5, 11, 4, 12, 3, 13, 2, 14, 1, 15)


def split_np(table):
    hi = table.astype(ml_dtypes.bfloat16)
    lo = (table - hi.astype(np.float64)).astype(ml_dtypes.bfloat16)
    return np.stack([hi, lo])


def n_of(p, z):
    return ((p % 16) // 4) * 128 + (z // 8) * 64 + (p // 16) * 32 + (p % 4) * 8 + z % 8


def k1_of(q, r):
    return (q % 4) * 128 + (r // 4) * 16 + (q // 4) * 4 + r % 4


def tables():
    idx = np.arange(512)
    n_rows = n_of(idx // 16, idx % 16)
    n_cols = n_of((idx % 256) // 8, (idx % 8) * 2 + idx // 256)
    k_rows = k1_of(idx // 32, idx % 32)
    k_cols = k1_of((idx % 256) // 16, (idx // 256) * 16 + idx % 16)

    def pair(rows, cols, factor):
        angle = (rows[:, None] * cols[None, :] % 512) * (2.0 * math.pi / 512)
        return np.cos(angle) * factor, np.sin(angle) * factor

    unit = 1.0 / math.sqrt(512.0)

    def by_rows(rows, cols, factor):
        c, s = pair(rows, cols, factor)
        return split_np(np.stack([c.reshape(4, 128, 512), s.reshape(4, 128, 512)], 1).reshape(1024, 512))

    first = by_rows(k_rows, n_cols, 2.0 * unit)
    last = by_rows(n_rows, k_cols, 0.5 * unit)
    c, s = pair(idx, idx, unit)
    mid = split_np(np.stack([c.reshape(512, 4, 128), s.reshape(512, 4, 128)], 2).reshape(512, 1024))
    return first, mid, last


def cross(first, second, bit, size):
    low = jnp.where(bit, pltpu.roll(second, size, 1), first)
    high = jnp.where(bit, second, pltpu.roll(first, 128 - size, 1))
    return low, high


def split(value):
    hi = value.astype(BF16)
    return hi, (value - hi.astype(F32)).astype(BF16)


def dot(a, b):
    return jnp.dot(a, b, preferred_element_type=F32)


def kernel(
    x_re, x_im, gate, cot_re, cot_im, filt_re, filt_im, first_hbm, mid_hbm, last_hbm,
    outs,
    vx_re, vx_im, vgate, vcot_re, vcot_im, first, mid, last, tw_cos, tw_sin, bend_cos, bend_sin,
    z_out, z_in, p_in, part, xx, k_out, k_in, dd, g_keep, f_mid, f_in, df_out, df_mid, ee, m_out, m_in, xx2, g_out, g_in, v_out, v_in, dfilt,
    in_sem, tab_sem, send, recv,
):
    grp = lax.axis_index("grp")
    seq = lax.axis_index("seq")
    x, zh, c = grp // 4, (grp // 2) % 2, grp % 2
    y, zl = seq // 8, seq % 8
    z = zh * 8 + zl
    xc = x * 2 + c
    q = x * 4 + y
    p = c * 16 + q
    near = z % 2
    far = 1 - near

    def dev(p_to, z_to):
        return (((p_to // 4) % 4) * 4 + (z_to // 8) * 2 + p_to // 16, (p_to % 4) * 8 + z_to % 8)

    bar = pltpu.get_barrier_semaphore()

    def greet(p_to, z_to):
        pl.semaphore_signal(bar, inc=1, device_id=dev(p_to, z_to), device_id_type=MESH)

    loads = [
        pltpu.make_async_copy(src, dst, in_sem.at[i])
        for i, (src, dst) in enumerate(
            ((x_re, vx_re), (x_im, vx_im), (gate, vgate), (cot_re, vcot_re), (cot_im, vcot_im))
        )
    ]
    for load in loads:
        load.start()
    for off in Z_ORDER:
        greet(p, (z + off) % 16)
    for off in range(31, 0, -1):
        greet(p ^ off, z)
    table_loads = [
        pltpu.make_async_copy(src, dst, tab_sem.at[i])
        for i, (src, dst) in enumerate(((first_hbm, first), (mid_hbm, mid), (last_hbm, last)))
    ]
    for load in table_loads:
        load.start()

    lane = lax.broadcasted_iota(jnp.int32, (32, 128), 1)
    row = lax.broadcasted_iota(jnp.int32, (32, 128), 0)
    bit6 = (lane & 64) != 0
    bit5 = (lane & 32) != 0

    for load in loads:
        load.wait()
    for t in range(4):
        cols = pl.ds(t * 128, 128)
        g = vgate[:, cols]
        a = [vx_re[:, cols] * g, vcot_re[:, cols], vx_im[:, cols] * g, vcot_im[:, cols]]
        b = [None] * 4
        b[0], b[2] = cross(a[0], a[2], bit6, 64)
        b[1], b[3] = cross(a[1], a[3], bit6, 64)
        w = [None] * 4
        w[0], w[1] = cross(b[0], b[1], bit5, 32)
        w[2], w[3] = cross(b[2], b[3], bit5, 32)
        for i in range(4):
            for tile in range(4):
                z_out[pl.ds(tile * 128 + i * 4 + t, 8, stride=16), :] = w[i][tile * 8 : tile * 8 + 8]

    pl.semaphore_wait(bar, 46)

    def z_rows(z_to):
        return (z_to % 8) // 2, (z_to // 8) * 4 + (z_to % 2) * 2

    for off in Z_ORDER:
        stage = 0 if off % 2 else 10
        z_to = (z + off) % 16
        tile, sub = z_rows(z_to)
        pltpu.make_async_remote_copy(
            z_out.at[pl.ds(tile * 128 + sub * 16, 32), :], z_in.at[near, z // 2],
            send.at[stage], recv.at[stage], device_id=dev(p, z_to), device_id_type=MESH,
        ).start()
    tile, sub = z_rows(z)
    pltpu.make_async_copy(z_out.at[pl.ds(tile * 128 + sub * 16, 32), :], z_in.at[near, z // 2], recv.at[10]).start()

    def own_rows(k):
        return pl.ds(4 * k, 4)

    def plane_step(stage, moves):
        for off in (7, 5, 3, 6, 4, 2, 1, 0):
            other = xc ^ off
            for src, dst in moves(other // 2, other % 2, other):
                if off:
                    pltpu.make_async_remote_copy(
                        src, dst, send.at[stage], recv.at[stage],
                        device_id=dev((other % 2) * 16 + (other // 2) * 4 + y, z), device_id_type=MESH,
                    ).start()
                else:
                    pltpu.make_async_copy(src, dst, recv.at[stage]).start()

    def line_step(src, dst, stage):
        for off in range(7, 0, -1):
            pltpu.make_async_remote_copy(
                src.at[:, own_rows(zl ^ off), :], dst.at[:, own_rows(zl), :],
                send.at[stage], recv.at[stage], device_id=dev(p, z ^ off), device_id_type=MESH,
            ).start()
        pltpu.make_async_copy(src.at[:, own_rows(zl), :], dst.at[:, own_rows(zl), :], recv.at[stage]).start()

    plane_step(
        6,
        lambda x_to, c_to, xc_to: (
            (filt_re.at[c_to, own_rows(x_to), :], f_mid.at[0, own_rows(xc), :]),
            (filt_im.at[c_to, own_rows(x_to), :], f_mid.at[1, own_rows(xc), :]),
        ),
    )

    def angles(k, m):
        return (k * m).astype(F32) * (2.0 * math.pi / SEQ)

    sign = jnp.where(lax.broadcasted_iota(jnp.int32, (128, 128), 1) < 64, 1.0, -1.0).astype(F32)
    m_lane = lax.broadcasted_iota(jnp.int32, (128, 128), 1) % 32 + (y * 128 + x * 32)
    for i in range(4):
        k_row = lax.broadcasted_iota(jnp.int32, (128, 128), 0) + i * 128
        theta = angles(k1_of(k_row // 32, k_row % 32), m_lane)
        tw_cos[pl.ds(i * 128, 128), :] = jnp.cos(theta)
        tw_sin[pl.ds(i * 128, 128), :] = jnp.sin(theta) * sign
        theta = angles(k1_of(q, row), lane + i * 128)
        bend_cos[:, pl.ds(i * 128, 128)] = jnp.cos(theta)
        bend_sin[:, pl.ds(i * 128, 128)] = jnp.sin(theta)

    def plane(src, dst, stage, offs, own):
        for off in offs:
            pltpu.make_async_remote_copy(
                src.at[p ^ off], dst.at[p], send.at[stage], recv.at[stage],
                device_id=dev(p ^ off, z), device_id_type=MESH,
            ).start()
        if own:
            pltpu.make_async_copy(src.at[p], dst.at[p], recv.at[stage]).start()

    def chips(src, dst, stage, offs, own):
        for off in offs:
            pltpu.make_async_remote_copy(
                src.at[q ^ off], dst.at[q], send.at[stage], recv.at[stage],
                device_id=dev(p ^ off, z), device_id_type=MESH,
            ).start()
        if own:
            pltpu.make_async_copy(src.at[q], dst.at[q], recv.at[stage]).start()

    halves = ((far, 0, 1), (near, 10, 11))
    for half, got, stage in halves:
        pltpu.make_async_copy(z_in.at[half], z_in.at[half], recv.at[got]).wait()
        for off in (26, 22, 25, 27, 30, 10, 18, 21, 23, 24, 29, 31, 6, 9, 11, 14, 17, 19, 20, 28, 2, 5, 7, 8, 13, 15, 16, 1, 3, 4, 12):
            pltpu.make_async_remote_copy(
                z_in.at[half, :, p ^ off], p_in.at[half, p], send.at[stage], recv.at[stage],
                device_id=dev(p ^ off, z), device_id_type=MESH,
            ).start()
        pltpu.make_async_copy(z_in.at[half, :, p], p_in.at[half, p], recv.at[stage]).start()
    pltpu.make_async_copy(f_mid, f_mid, recv.at[6]).wait()
    line_step(f_mid, f_in, 7)

    table_loads[0].wait()
    for at, (half, got, stage) in enumerate(halves):
        pltpu.make_async_copy(p_in.at[half], p_in.at[half], recv.at[stage]).wait()
        hi, lo = split(p_in[half].reshape(256, 128))
        xx[at, :, :128] = hi
        xx[at, :, 128:] = lo
        depth = pl.ds(pl.multiple_of(half * 256, 256), 256)
        for i in range(4):
            chunk = (q // 4) ^ i
            rows = pl.ds(pl.multiple_of(chunk * 256, 256), 256)
            out = dot(first[0, rows, depth], xx[at]) + dot(first[1, rows, depth], xx[at])
            acc = out[:, :128] + out[:, 128:]
            if at == 0:
                part[i] = acc
                continue
            acc = acc + part[i]
            spec = acc[:128] + sign * pltpu.roll(acc[128:], 64, 1)
            rows = pl.ds(pl.multiple_of(chunk * 128, 128), 128)
            turned = spec * tw_cos[rows, :] + pltpu.roll(spec, 64, 1) * tw_sin[rows, :]
            k_out[pl.ds(chunk * 4, 4)] = turned.reshape(4, 32, 128)
            chips(k_out, k_in, 2, range(i * 4 + (i == 0), i * 4 + 4), i == 0)

    table_loads[1].wait()
    pltpu.make_async_copy(k_in, k_in, recv.at[2]).wait()

    for t in range(4):
        cols = pl.ds(t * 128, 128)
        a = [cross(k_in[w1 * 4 + t], k_in[8 + w1 * 4 + t], bit6, 64) for w1 in range(2)]
        for ri in range(2):
            b = cross(a[0][ri], a[1][ri], bit5, 32)
            for ug in range(2):
                hi, lo = split(b[ug])
                dd[ug, pl.ds(ri * 32, 32), cols] = hi
                dd[ug, pl.ds(64 + ri * 32, 32), cols] = lo

    def spectrum(which, i):
        wide = pl.ds(i * 256, 256)
        out = dot(dd[which], mid[0, :, wide]) + dot(dd[which], mid[1, :, wide])
        acc = out[:64] + out[64:]
        return acc[:32, :128] + acc[32:, 128:], acc[32:, :128] - acc[:32, 128:]

    pltpu.make_async_copy(f_in, f_in, recv.at[7]).wait()
    for i in range(4):
        cols = pl.ds(i * 128, 128)
        g_re, g_im = spectrum(1, i)
        g_keep[0, :, cols] = g_re
        g_keep[1, :, cols] = g_im
        f_re = f_in[0, :, cols]
        f_im = f_in[1, :, cols]
        hi, lo = split(jnp.concatenate([f_re * g_re + f_im * g_im, f_re * g_im - f_im * g_re], 0))
        ee[:64, cols] = hi
        ee[64:, cols] = lo

    mask5 = bit5[:16]
    for t in range(4):
        wide = pl.ds(t * 256, 256)
        cols = pl.ds(t * 128, 128)
        out = dot(ee[...], mid[0, :, wide]) + dot(ee[...], mid[1, :, wide])
        acc = out[:64] + out[64:]
        re = acc[:32, :128] - acc[32:, 128:]
        im = acc[32:, :128] + acc[:32, 128:]
        b_cos, b_sin = bend_cos[:, cols], bend_sin[:, cols]
        bent = cross(re * b_cos - im * b_sin, im * b_cos + re * b_sin, bit6, 64)
        for w2 in range(2):
            d = cross(bent[w2][:16], bent[w2][16:], mask5, 32)
            for w1 in range(2):
                m_out[w2 * 8 + w1 * 4 + t] = d[w1]

    chips(m_out, m_in, 3, range(15, 0, -1), True)

    for i in range(4):
        cols = pl.ds(i * 128, 128)
        u_re, u_im = spectrum(0, i)
        g_re, g_im = g_keep[0, :, cols], g_keep[1, :, cols]
        df_out[0, :, cols] = g_re * u_re + g_im * u_im
        df_out[1, :, cols] = g_im * u_re - g_re * u_im
    line_step(df_out, df_mid, 8)

    table_loads[2].wait()
    pltpu.make_async_copy(m_in, m_in, recv.at[3]).wait()

    v = m_in[...].reshape(256, 128)
    wide5 = (lax.broadcasted_iota(jnp.int32, (256, 128), 1) & 32) != 0
    hi, lo = split(jnp.where(wide5, pltpu.roll(v, 32, 1), v))
    xx2[:256, :128] = hi
    xx2[:256, 128:] = lo
    hi, lo = split(jnp.where(wide5, v, pltpu.roll(v, 96, 1)))
    xx2[256:, :128] = hi
    xx2[256:, 128:] = lo
    pick5 = (lax.broadcasted_iota(jnp.int32, (8, 8, 128), 2) & 32) != 0
    for i in range(4):
        chunk = (p // 8) ^ i
        rows = pl.ds(pl.multiple_of(chunk * 256, 256), 256)
        out = dot(last[0, rows, :], xx2[...]) + dot(last[1, rows, :], xx2[...])
        acc = out[:, :128] + out[:, 128:]
        g = (acc[:128] - sign * pltpu.roll(acc[128:], 64, 1)).reshape(8, 2, 8, 128)
        g_out[pl.ds(chunk * 8, 8)] = jnp.where(pick5, g[:, 1], g[:, 0])
        plane(g_out, g_in, 4, range(i * 8 + (i == 0), i * 8 + 8), i == 0)
    pltpu.make_async_copy(g_in, g_in, recv.at[4]).wait()

    for l in range(2):
        for w2 in range(2):
            at = l * 16 + w2 * 8
            a, b = g_in[pl.ds(at, 4)].reshape(32, 128), g_in[pl.ds(at + 4, 4)].reshape(32, 128)
            low, high = cross(a, b, bit5, 32)
            v_out[0, l, pl.ds(w2 * 4, 4)] = low.reshape(4, 8, 128)
            v_out[1, l, pl.ds(w2 * 4, 4)] = high.reshape(4, 8, 128)
    for off in Z_ORDER:
        z_to = (z + off) % 16
        for l in range(2):
            pltpu.make_async_remote_copy(
                v_out.at[z_to // 8, l, :, z_to % 8], v_in.at[tile, :, sub + l], send.at[5], recv.at[5],
                device_id=dev(p, z_to), device_id_type=MESH,
            ).start()
    for l in range(2):
        pltpu.make_async_copy(v_out.at[zh, l, :, zl], v_in.at[tile, :, sub + l], recv.at[5]).start()
    pltpu.make_async_copy(df_mid, df_mid, recv.at[8]).wait()
    plane_step(
        9, lambda x_to, c_to, xc_to: ((df_mid.at[:, own_rows(xc_to), :], dfilt.at[:, c, own_rows(x), :]),)
    )
    pltpu.make_async_copy(v_in, v_in, recv.at[5]).wait()

    for t in range(4):
        a = [v_in[:, w2 * 4 + t].reshape(32, 128) for w2 in range(2)]
        re, im = cross(a[0], a[1], bit6, 64)
        outs[0, :, pl.ds(t * 128, 128)] = re
        outs[1, :, pl.ds(t * 128, 128)] = im

    pltpu.make_async_copy(dfilt, dfilt, recv.at[9]).wait()
    outs[2:] = dfilt[...].reshape(2, 32, 512)

    def sent(ref, stage):
        pltpu.make_async_copy(ref, ref, send.at[stage]).wait()

    sent(z_in.at[0], 0)
    sent(z_in.at[0, pl.ds(0, 7)], 10)
    for stage in (1, 11):
        sent(p_in.at[0, pl.ds(0, 31)], stage)
    sent(k_in.at[pl.ds(0, 15)], 2)
    sent(m_in.at[pl.ds(0, 15)], 3)
    sent(g_in.at[pl.ds(0, 31)], 4)
    sent(g_in.at[pl.ds(0, 30)], 5)
    for stage in (6, 7, 8, 9):
        sent(m_in.at[pl.ds(0, 14)], stage)


def finish(x_re, x_im, gate, outs, dx_re, dx_im, dgate, dfilt_re, dfilt_im):
    dx_re[...] = gate[...] * outs[0]
    dx_im[...] = gate[...] * outs[1]
    dgate[...] = x_re[...] * outs[0] + x_im[...] * outs[1]
    dfilt_re[...] = (outs[2] * 0.25).reshape(2, 16, 512)
    dfilt_im[...] = (outs[3] * 0.25).reshape(2, 16, 512)


def per_device(x_re, x_im, gate_in, cot_re, cot_im, filt_re, filt_im):
    first, mid, last = (jnp.asarray(t) for t in tables())
    vm = pltpu.VMEM
    outs = pl.pallas_call(
        kernel,
        out_shape=jax.ShapeDtypeStruct((4, 32, 512), F32),
        in_specs=[pl.BlockSpec(memory_space=pl.ANY)] * 10,
        out_specs=pl.BlockSpec(memory_space=pltpu.VMEM),
        scratch_shapes=[
            vm((32, 512), F32), vm((32, 512), F32), vm((32, 512), F32), vm((32, 512), F32), vm((32, 512), F32),
            vm((2, 1024, 512), BF16), vm((2, 512, 1024), BF16), vm((2, 1024, 512), BF16),
            vm((512, 128), F32), vm((512, 128), F32), vm((32, 512), F32), vm((32, 512), F32),
            vm((512, 128), F32), vm((2, 8, 32, 128), F32), vm((2, 32, 8, 128), F32), vm((4, 256, 128), F32),
            vm((2, 256, 256), BF16), vm((16, 32, 128), F32), vm((16, 32, 128), F32), vm((2, 128, 512), BF16),
            vm((2, 32, 512), F32),
            vm((2, 32, 512), F32), vm((2, 32, 512), F32), vm((2, 32, 512), F32), vm((2, 32, 512), F32),
            vm((128, 512), BF16), vm((16, 16, 128), F32), vm((16, 16, 128), F32), vm((512, 256), BF16),
            vm((32, 8, 128), F32), vm((32, 8, 128), F32), vm((2, 2, 8, 8, 128), F32), vm((4, 8, 8, 128), F32),
            vm((2, 2, 16, 512), F32),
            pltpu.SemaphoreType.DMA((5,)), pltpu.SemaphoreType.DMA((3,)),
            pltpu.SemaphoreType.DMA((12,)), pltpu.SemaphoreType.DMA((12,)),
        ],
        name="spectral_backward",
        compiler_params=pltpu.CompilerParams(
            collective_id=0, has_side_effects=True, vmem_limit_bytes=60 * 1024 * 1024
        ),
    )(x_re, x_im, gate_in, cot_re, cot_im, filt_re, filt_im, first, mid, last)
    vmem = pl.BlockSpec(memory_space=pltpu.VMEM)
    wide = jax.ShapeDtypeStruct((32, 512), F32)
    return pl.pallas_call(
        finish,
        out_shape=(wide, wide, wide) + (jax.ShapeDtypeStruct(filt_re.shape, F32),) * 2,
        in_specs=[vmem] * 4,
        out_specs=(vmem,) * 5,
        name="products",
    )(x_re, x_im, gate_in, outs)


def solution(mesh):
    seq_in = P(None, ("grp", "seq"))
    filt = P("grp", "seq", None)
    return jax.shard_map(
        per_device,
        mesh=mesh,
        in_specs=(seq_in,) * 5 + (filt,) * 2,
        out_specs=(seq_in,) * 3 + (filt,) * 2,
        check_vma=False,
    )
```
